256 devices in a mesh: group: 8 (over y, core), owner: 32 (over x, z).
Axes of the slice: x: 4, y: 4, z: 8, core: 2. Of those that a mesh axis runs over, the one named last changes fastest.
Arguments:
- first_table: float32 [8, 16384, 400], P('group', 'owner'), may hold values from -1.5 to 1.5
- first_state: float32 [8, 16384], P('group', 'owner'), may hold values from 0.001 to 0.01
- second_table: float32 [8, 16384, 400], P('group', 'owner'), may hold values from -1.5 to 1.5
- second_state: float32 [8, 16384], P('group', 'owner'), may hold values from 0.001 to 0.01
- relation_diag: float32 [2304, 400], replicated, may hold values from 0.5 to 1.5
- relation_state: float32 [2304], replicated, may hold values from 0.001 to 0.01
- source_row: int32 [8, 32768], P('group', 'owner'), may hold values from 0 to 511
- target_owner: int32 [8, 32768, 1], P('group', 'owner'), may hold values from 0 to 31; in each aligned block of 1024 rows (0 to 1023, 1024 to 2047, ..., all dimensions but the last counted through in order) at most 80 rows name the same one
- target_row: int32 [8, 32768], P('group', 'owner'), may hold values from 0 to 511
- relation_id: int32 [8, 32768], P('group', 'owner'), may hold values from 0 to 2303
- negative_id: int32 [8, 2, 100], P('group'), may hold values from 0 to 16383
Outputs:
- first_new: float32 [8, 16384, 400], P('group', 'owner')
- first_state_new: float32 [8, 16384], P('group', 'owner')
- second_new: float32 [8, 16384, 400], P('group', 'owner')
- second_state_new: float32 [8, 16384], P('group', 'owner')
- relation_new: float32 [2304, 400], replicated
- relation_state_new: float32 [2304], replicated
The draws below stay inside these ranges and needn't reach their ends.
Inputs may be any that keep to these rules, and one draw needn't show every extreme that they name: `target_owner`: among the edges of one device, at most 80 name the same owner, and some device reaches 80.
All inputs are finite; a program needn't handle non-finite values.
Results may differ from the reference program's by a relative error of at most 0.0034.
The reference program's roundings to bfloat16 on the way count: a program that leaves them out, or rounds other values in their place, can miss the bound.
Values may be sent and summed in bfloat16 or wider, within the bound.
A program may use at most 128 MiB of HBM per device.

```python
import math
import jax
import jax.numpy as jnp
import numpy as np
from jax import lax

D = 400
REL = 2304
NEG = 100
BLOCK = 512
R_DEV = 512
E_DEV = 1024
CAP = 80
BLOCKS = 2
PART_ROWS = 16384
EDGES = 32768
N_GROUP = 8
N_OWNER = 32


def touch_ends(entries, key, least, top_value):
    longest = entries.shape.index(max(entries.shape))
    spots = []
    for shift in (0, 1):
        where = [jax.random.randint(jax.random.fold_in(key, axis), (), 0, length) for axis, length in enumerate(entries.shape)]
        where[longest] = (where[longest] + shift) % entries.shape[longest]
        spots.append(tuple(where))
    return entries.at[spots[0]].set(least).at[spots[1]].set(top_value)


def levels(rng, dims, cuts, smallest, high):
    gain, own = 1.0, jax.random.fold_in(rng, 6)
    for axis_at, blocks in cuts:
        draws = jnp.exp(jax.random.uniform(jax.random.fold_in(own, axis_at), (blocks,), jnp.float32, smallest / len(cuts), high / len(cuts)))
        gain = gain * jnp.repeat(draws, dims[axis_at] // blocks).reshape([-1 if axis == axis_at else 1 for axis in range(len(dims))])
    return gain


def cumulative_ranks(amount, slope):
    portions = [(1 << 20) // math.isqrt(rank ** slope) + 1 for rank in range(1, amount + 1)]
    spread = 1 + sum(portions) // (1 << 30)
    return np.cumsum(np.array([max(1, weight // spread) for weight in portions]))


def ranked_ids(own_key, dims, number_of, lean):
    listing = cumulative_ranks(number_of, lean)
    ticket = jax.random.randint(jax.random.fold_in(own_key, 1), dims, 0, int(listing[number_of - 1]))
    standing = jnp.searchsorted(jnp.asarray(listing, jnp.int32), ticket, side="right")
    return jax.random.permutation(jax.random.fold_in(own_key, 2), number_of)[standing].astype(jnp.int32)


def routed_block(rng, own, number, rows, amount, top, reach, skew):
    ranking = jax.random.permutation(rng, amount)
    crowded, common = shares(amount, rows * top, reach, skew, True), shares(amount, rows * top, reach, skew, False)
    places = jnp.arange(amount)

    def named(lengths, rotation):
        used = int((lengths > 0).sum())
        fixed = max(1, used // 4)
        passed = fixed + (places - fixed + rotation * (used - fixed)) % max(1, amount - fixed)
        return jnp.zeros((amount,), jnp.int32).at[ranking[jnp.where(places < fixed, places, passed)]].set(jnp.asarray(lengths, jnp.int32))

    lengths = jnp.where(number % 4 == 0, named(crowded, number // 4), named(common, number - number // 4 - 1))
    mixed = jax.random.permutation(jax.random.fold_in(own, 3), amount)
    donor, taker = mixed[0:amount // 2 * 2:2], mixed[1:amount // 2 * 2:2]
    margin = jnp.minimum(lengths[donor] - 1, reach - lengths[taker]) // 2
    margin = jnp.where((donor == ranking[0]) | (taker == ranking[0]) | (lengths[taker] == 0), 0, jnp.maximum(margin, 0))
    passed = jax.random.randint(jax.random.fold_in(own, 4), (amount // 2,), 0, 1 << 20) % (margin + 1)
    lengths = lengths.at[donor].add(-passed).at[taker].add(passed)
    members = jnp.searchsorted(jnp.cumsum(lengths), jnp.arange(rows * top), side="right").astype(jnp.int32)
    table = members.reshape(top, rows).T
    table = table[jax.random.permutation(jax.random.fold_in(own, 1), rows)]
    rotation = jax.random.randint(jax.random.fold_in(own, 2), (rows, 1), 0, top)
    return jnp.take_along_axis(table, (jnp.arange(top)[None, :] + rotation) % top, axis=1)


def shares(count, total, limit, lean, full):
    portions = [(1 << 20) // math.isqrt(rank ** lean) + 1 for rank in range(1, count + 1)]
    largest = limit if full else min(limit, max(-(-total // count), total * portions[0] // sum(portions)))
    least = 1 if total - largest >= count - 1 else 0
    counts, spare = [largest] + [least] * (count - 1), total - largest - least * (count - 1)
    while spare > 0:
        candidates = [i for i in range(1, count) if counts[i] < largest] or [i for i in range(1, count) if counts[i] < limit]
        pool, left = sum([portions[i] for i in candidates]), spare
        for i in candidates:
            more = min(limit - counts[i], max(1, left * portions[i] // pool), spare)
            counts[i] = counts[i] + more
            spare = spare - more
    return np.array(counts)


def noise(rng, dims, scale, reach, pieces=(), kind=jnp.bfloat16):
    array = jax.random.normal(rng, dims, jnp.float32) * scale
    if len(pieces) > 0:
        array = levels(rng, dims, pieces, -0.22, 0.18) * array
    return jnp.clip(array, min=-reach, max=reach).astype(kind)


def setup_inputs(seed: int = 0) -> dict:
    keys = jax.random.split(jax.random.key(seed), 12)
    first_table = noise(keys[0], (N_GROUP, PART_ROWS, D), 0.25, 1.5, ((0, 8), (1, 32)), jnp.float32)
    first_state = jnp.clip(jnp.exp(math.log(0.01) - 2.30258502 * jax.random.uniform(keys[1], (N_GROUP, PART_ROWS), jnp.float32) ** levels(keys[1], (N_GROUP, PART_ROWS), ((0, 8), (1, 32)), -0.2, 0.2)), 0.001, 0.01)
    second_table = noise(keys[2], (N_GROUP, PART_ROWS, D), 0.25, 1.5, ((0, 8), (1, 32)), jnp.float32)
    second_state = jnp.clip(jnp.exp(math.log(0.01) - 2.30258502 * jax.random.uniform(keys[3], (N_GROUP, PART_ROWS), jnp.float32) ** levels(keys[3], (N_GROUP, PART_ROWS), ((0, 8), (1, 32)), -0.2, 0.2)), 0.001, 0.01)
    relation_diag = jnp.clip(1.0 + 0.1 * jax.random.normal(keys[4], (REL, D), jnp.float32), 0.5, 1.5)
    relation_state = jnp.clip(jnp.exp(jax.random.uniform(keys[5], (REL,), jnp.float32, math.log(0.001), math.log(0.01))), 0.001, 0.01)
    source_row = touch_ends(jax.random.randint(keys[6], (N_GROUP, EDGES), 0, R_DEV), jax.random.fold_in(keys[6], 1), 0, R_DEV - 1).astype(jnp.int32)
    target_owner_keys = jax.random.split(jax.random.fold_in(keys[7], 1), N_GROUP * EDGES // E_DEV)
    target_owner_turns = jax.random.permutation(jax.random.fold_in(keys[7], 3), N_GROUP * EDGES // E_DEV)
    target_owner = jax.vmap(lambda own, number: routed_block(jax.random.fold_in(keys[7], 2), own, number, E_DEV, N_OWNER, 1, CAP, 2))(target_owner_keys, target_owner_turns).reshape((N_GROUP, EDGES, 1))
    target_row = touch_ends(jax.random.randint(keys[8], (N_GROUP, EDGES), 0, R_DEV), jax.random.fold_in(keys[8], 1), 0, R_DEV - 1).astype(jnp.int32)
    relation_id = touch_ends(ranked_ids(keys[9], (N_GROUP, EDGES), REL, 2), jax.random.fold_in(keys[9], 3), 0, REL - 1).astype(jnp.int32)
    negative_id = touch_ends(jax.random.randint(keys[10], (N_GROUP, BLOCKS, NEG), 0, PART_ROWS), jax.random.fold_in(keys[10], 1), 0, PART_ROWS - 1).astype(jnp.int32)
    return {"first_table": first_table, "first_state": first_state, "second_table": second_table, "second_state": second_state, "relation_diag": relation_diag, "relation_state": relation_state, "source_row": source_row, "target_owner": target_owner, "target_row": target_row, "relation_id": relation_id, "negative_id": negative_id}


learn_rate = 0.1

def adagrad_rows(table, state, grad):
    state_new = state + lax.optimization_barrier(jnp.mean(grad * grad, axis=-1))
    return (table - learn_rate * grad / jnp.sqrt(state_new)[:, None], state_new)

def group_bucket(src_table, dst_table, relation_diag, src_row, dst_owner, dst_row, kinds, negatives):
    src_copy = src_table.astype(jnp.bfloat16)
    dst_copy = dst_table.astype(jnp.bfloat16)
    holder = (jnp.arange(EDGES, dtype=jnp.int32) // E_DEV).astype(jnp.int32)
    src_index = (holder * R_DEV + src_row).astype(jnp.int32)
    dst_index = (dst_owner * R_DEV + dst_row).astype(jnp.int32)
    src_rows = src_copy[src_index]
    dst_rows = dst_copy[dst_index]
    neg_rows = dst_copy[negatives]
    rel_rows = relation_diag[kinds]
    queries = (src_rows.astype(jnp.float32) * rel_rows).astype(jnp.bfloat16)
    count = EDGES // BLOCK
    query_blocks = queries.reshape(count, BLOCK, D).astype(jnp.float32)
    target_blocks = dst_rows.reshape(count, BLOCK, D).astype(jnp.float32)
    block_index = jnp.arange(count, dtype=jnp.int32) % BLOCKS
    neg_blocks = neg_rows[block_index].astype(jnp.float32)
    batch = jnp.einsum('kcd,kjd->kcj', query_blocks, target_blocks)
    sampled = jnp.einsum('kcd,knd->kcn', query_blocks, neg_blocks)
    scale = 1.0 / (BLOCK - 1 + NEG)
    diagonal = jnp.eye(BLOCK, dtype=bool)[None]
    d_batch = jnp.where(diagonal, -jax.nn.sigmoid(-batch), scale * jax.nn.sigmoid(batch)).astype(jnp.bfloat16).astype(jnp.float32)
    d_sampled = (scale * jax.nn.sigmoid(sampled)).astype(jnp.bfloat16).astype(jnp.float32)
    d_query = jnp.einsum('kcj,kjd->kcd', d_batch, target_blocks) + jnp.einsum('kcn,knd->kcd', d_sampled, neg_blocks)
    d_target = jnp.einsum('kcj,kcd->kjd', d_batch, query_blocks).astype(jnp.bfloat16).reshape(EDGES, D)
    d_negative = jnp.einsum('kcn,kcd->knd', d_sampled, query_blocks).reshape(N_OWNER, BLOCKS, NEG, D).sum(axis=0)
    d_query = d_query.reshape(EDGES, D)
    d_source = (d_query * rel_rows).astype(jnp.bfloat16)
    d_relation = jax.ops.segment_sum(d_query * src_rows.astype(jnp.float32), kinds, num_segments=REL)
    src_grad = jax.ops.segment_sum(d_source.astype(jnp.float32), src_index, num_segments=PART_ROWS)
    dst_grad = jax.ops.segment_sum(d_target.astype(jnp.float32), dst_index, num_segments=PART_ROWS)
    dst_grad = dst_grad + jax.ops.segment_sum(d_negative.reshape(BLOCKS * NEG, D), negatives.reshape(-1), num_segments=PART_ROWS)
    return (src_grad, dst_grad, d_relation)

def reference(first_table, first_state, second_table, second_state, relation_diag, relation_state, source_row, target_owner, target_row, relation_id, negative_id):
    rel_total = jnp.zeros((REL, D), jnp.float32)
    firsts = []
    seconds = []
    for g in range(N_GROUP):
        src_grad, dst_grad, d_relation = group_bucket(first_table[g], second_table[g], relation_diag, source_row[g], target_owner[g, :, 0], target_row[g], relation_id[g], negative_id[g])
        rel_total = rel_total + d_relation
        firsts.append(adagrad_rows(first_table[g], first_state[g], src_grad))
        seconds.append(adagrad_rows(second_table[g], second_state[g], dst_grad))
    relation_new, relation_state_new = adagrad_rows(relation_diag, relation_state, rel_total)
    return (jnp.stack([item[0] for item in firsts]), jnp.stack([item[1] for item in firsts]), jnp.stack([item[0] for item in seconds]), jnp.stack([item[1] for item in seconds]), relation_new, relation_state_new)
```

```python
import jax
import jax.numpy as jnp
from jax import lax
from jax.experimental import pallas as pl
from jax.experimental.pallas import tpu as pltpu
from jax.sharding import PartitionSpec as P

MESH = pl.DeviceIdType.MESH
F32 = jnp.float32
BF16 = jnp.bfloat16
LEARN = 0.1

D = 400
R = 512
E = 1024
BLOCK = 512
NEG = 100
NL = 128
K = 2304
NX, NY, NZ = 4, 4, 8
SLOTS = 256

GROUPS = ((0, 1, 7), (2, 6), (3, 5, 4))
CUTS = ((0, 96), (96, 112), (208, 96), (304, 96))
UP = (0, 7, 6, 5, 4)
DOWN = (0, 1, 2, 3, 4)
HALF = 208

H_CORE, H_Y, H_X, H_Z = 4096, 1024, 256, 32

NN = (((1,), (0,)), ((), ()))
NT = (((1,), (1,)), ((), ()))
TN = (((0,), (0,)), ((), ()))


def dot(a, b, dims):
    return lax.dot_general(a, b, dims, preferred_element_type=F32)


def onehot(vec, base, n):
    rows = lax.broadcasted_iota(jnp.int32, (n, vec.shape[1]), 0)
    return jnp.where(rows == vec - base, 1.0, 0.0).astype(BF16)


def adagrad(table, state, grad):
    state_new = state + jnp.sum(grad * grad, axis=0, keepdims=True) * (1.0 / D)
    return table - LEARN * grad * (1.0 / jnp.sqrt(state_new)), state_new


def step_kernel(
    first_ref, fstate_ref, second_ref, sstate_ref, diag_ref,
    srow_ref, towner_ref, trow_ref, kind_ref, neg_ref,
    first_new, fstate_new, second_new, sstate_new, rel_out,
    tabs, req, asked, serve, back, negpart, place_ref,
    splits, relrow, srcrow, query, dst, summand, dsource, dtarget, dneg, dnegpart,
    csend, crecv, up_send, up_recv, down_send, down_recv,
    relbuf, core_recv, y_recv, x_recv, z_recv, red_y, red_x,
    ag_s, ag_r, rq_s, rq_r, sv_s, sv_r, ng_s, ng_r, cs_s, cs_r, dn_s, dn_r, rs_s, rs_r,
    co_s, co_r, ry_s, ry_r, rx_s, rx_r, rz_s, rz_r,
):
    g = lax.axis_index("group")
    o = lax.axis_index("owner")
    x, z = o // NZ, o % NZ
    y, c = g // 2, g % 2

    def dev_x(k):
        return (g, lax.rem(x + k, NX) * NZ + z)

    def dev_z(k):
        return (g, x * NZ + lax.rem(z + k, NZ))

    def dev_y(k):
        return (lax.rem(y + k, NY) * 2 + c, o)

    dev_c = (y * 2 + 1 - c, o)

    barrier = pltpu.get_barrier_semaphore()
    for peer in [dev_x(k) for k in range(1, NX)] + [dev_z(k) for k in range(1, NZ)] + [
        dev_y(k) for k in range(1, NY)
    ] + [dev_c]:
        pl.semaphore_signal(barrier, inc=1, device_id=peer, device_id_type=MESH)
    tabs[0] = second_ref[...].astype(BF16)
    pl.semaphore_wait(barrier, NX + NZ + NY - 3 + 1)

    def remote(src, dst_, ss, rs, dev):
        return pltpu.make_async_remote_copy(
            src_ref=src, dst_ref=dst_, send_sem=ss, recv_sem=rs, device_id=dev, device_id_type=MESH
        )

    def gather_copy(way, step, q):
        path = UP if way == 0 else DOWN
        rows = pl.ds(*CUTS[q])
        return remote(
            tabs.at[path[step], rows], tabs.at[path[step + 1], rows],
            ag_s.at[way, step, q], ag_r.at[way, step, q], dev_z(1 if way == 0 else NZ - 1),
        )

    def gather_cuts(way, step):
        return range(4) if step < 3 else ((0, 1) if way == 0 else (2, 3))

    for q in range(4):
        for way in (0, 1):
            gather_copy(way, 0, q).start()

    def forward(step):
        for q in range(4):
            for way in (0, 1):
                if q in gather_cuts(way, step):
                    gather_copy(way, step, q).wait_recv()
                    if step < 3 and q in gather_cuts(way, step + 1):
                        gather_copy(way, step + 1, q).start()

    towner, trow = towner_ref[...], trow_ref[...]
    far = lax.rem(towner % NZ - z + NZ, NZ)
    side = lax.rem(towner // NZ - x + NX, NX)
    group = jnp.zeros_like(far)
    local = jnp.zeros_like(far)
    for gi, members in enumerate(GROUPS):
        for li, offset in enumerate(members):
            group = jnp.where(far == offset, gi, group)
            local = jnp.where(far == offset, li, local)
    kind_of = side * 8 + group
    mine = jnp.where(lax.broadcasted_iota(jnp.int32, (32, E), 0) == kind_of, 1.0, 0.0)
    before_mask = jnp.where(
        lax.broadcasted_iota(jnp.int32, (E, E), 0) < lax.broadcasted_iota(jnp.int32, (E, E), 1), 1.0, 0.0
    ).astype(BF16)
    before = dot(mine.astype(BF16), before_mask, NN)
    slot = jnp.sum(mine * before, axis=0, keepdims=True).astype(jnp.int32)
    place_ref[...] = kind_of * SLOTS + slot
    value = local * R + trow + 1
    high = (value // 16).astype(F32)
    low = (value % 16).astype(F32)
    sends = jnp.concatenate([mine * high, mine * low], axis=0).astype(BF16)
    found = dot(sends, onehot(slot, 0, SLOTS), NT)
    wanted = (found[0:32] * 16.0 + found[32:64]).astype(jnp.int32) - 1
    asked[0] = wanted[0:8]
    for k in range(1, NX):
        req[k] = wanted[8 * k : 8 * k + 8]

    def req_copy(k):
        return remote(req.at[k], asked.at[NX - k], rq_s.at[k], rq_r.at[NX - k], dev_x(k))

    for k in range(1, NX):
        req_copy(k).start()

    first_copy = first_ref[...].astype(BF16)
    for b in range(2):
        lanes = slice(b * BLOCK, (b + 1) * BLOCK)
        srcrow[:, lanes] = dot(first_copy, onehot(srow_ref[:, lanes], 0, R), NN).astype(BF16)
    diag = diag_ref[...]
    high_part = diag.astype(BF16)
    rest = diag - high_part.astype(F32)
    splits[0] = high_part
    splits[1] = rest.astype(BF16)
    splits[2] = (rest - splits[1].astype(F32)).astype(BF16)

    for k in range(1, NX):
        remote(req.at[k], asked.at[k], rq_s.at[k], rq_r.at[k], dev_x(k)).wait_recv()

    def serve_copy(j, gi):
        return remote(
            serve.at[j, gi], back.at[NX - j, gi], sv_s.at[j, gi], sv_r.at[NX - j, gi], dev_x(j)
        )

    def serve_rows(j, gi):
        want = asked[j][gi : gi + 1, :]
        total = None
        for li, offset in enumerate(GROUPS[gi]):
            part = dot(tabs[offset], onehot(want, li * R, R), NN)
            total = part if total is None else total + part
        return total.astype(BF16)

    def serve_group(gi):
        def body(j, carry):
            serve[j, gi] = serve_rows(j, gi)
            serve_copy(j, gi).start()
            return carry

        lax.fori_loop(1, NX, body, 0)
        back[0, gi] = serve_rows(0, gi)

    def relation_rows(n):
        def body(i, carry):
            lanes = pl.ds(pl.multiple_of(i * 128, 128), 128)
            pick = onehot(kind_ref[:, lanes], 0, K)
            relrow[:, lanes] = (
                dot(splits[0], pick, NN) + dot(splits[1], pick, NN) + dot(splits[2], pick, NN)
            )
            return carry

        lax.fori_loop(n * 4, n * 4 + 4, body, 0)

    def wait_back(gi):
        for k in range(1, NX):
            remote(serve.at[k, gi], back.at[k, gi], sv_s.at[k, gi], sv_r.at[k, gi], dev_x(k)).wait_recv()

    def collect(gi, first):
        for b in range(2):
            lanes = slice(b * BLOCK, (b + 1) * BLOCK)

            def body(k, total):
                pick = onehot(place_ref[:, lanes], (k * 8 + gi) * SLOTS, SLOTS)
                return total + dot(back[k, gi], pick, NN)

            start = jnp.zeros((D, BLOCK), F32) if first else dst[:, lanes].astype(F32)
            dst[:, lanes] = lax.fori_loop(0, NX, body, start).astype(BF16)

    forward(0)
    serve_group(0)
    relation_rows(0)
    forward(1)
    serve_group(1)
    relation_rows(1)
    query[...] = (srcrow[...].astype(F32) * relrow[...]).astype(BF16)
    forward(2)
    forward(3)

    negs = neg_ref[...] - x * (NZ * R)
    line = jnp.zeros((D, 2 * NL), F32)
    for offset in range(NZ):
        line = line + dot(tabs[offset], onehot(negs, lax.rem(z + offset, NZ) * R, R), NN)
    negpart[0] = line.astype(BF16)

    def neg_copy(k):
        return remote(negpart.at[0], negpart.at[NX - k], ng_s.at[k], ng_r.at[NX - k], dev_x(k))

    serve_group(2)
    for k in range(1, NX):
        neg_copy(k).start()
    wait_back(0)
    collect(0, True)
    wait_back(1)
    collect(1, False)
    wait_back(2)
    collect(2, False)
    for k in range(1, NX):
        remote(negpart.at[0], negpart.at[k], ng_s.at[k], ng_r.at[k], dev_x(k)).wait_recv()
    negrow = (
        negpart[0].astype(F32) + negpart[1].astype(F32) + negpart[2].astype(F32) + negpart[3].astype(F32)
    ).astype(BF16)

    scale = 1.0 / (BLOCK - 1 + NEG)
    diagonal = lax.broadcasted_iota(jnp.int32, (BLOCK, BLOCK), 0) == lax.broadcasted_iota(
        jnp.int32, (BLOCK, BLOCK), 1
    )
    for b in range(2):
        lanes = slice(b * BLOCK, (b + 1) * BLOCK)
        nl = slice(b * NL, (b + 1) * NL)
        q, t, n = query[:, lanes], dst[:, lanes], negrow[:, nl]
        batch = dot(q, t, TN)
        sampled = dot(q, n, TN)
        d_batch = (
            jax.nn.sigmoid(jnp.where(diagonal, -batch, batch)) * jnp.where(diagonal, -1.0, scale)
        ).astype(BF16)
        d_sampled = (scale * jax.nn.sigmoid(sampled)).astype(BF16)
        d_query = dot(t, d_batch, NT) + dot(n, d_sampled, NT)
        dsource[:, lanes] = (d_query * relrow[:, lanes]).astype(BF16)
        summand[:, lanes] = (d_query * srcrow[:, lanes].astype(F32)).astype(BF16)
        dtarget[:, lanes] = dot(q, d_batch, NN).astype(BF16)
        dneg[:, nl] = dot(q, d_sampled, NN).astype(BF16)

    for half in range(2):
        relbuf[pl.ds(half * H_CORE + 3600, H_CORE - 3600)] = jnp.zeros((H_CORE - 3600, 128), BF16)

    def relation_part(i, carry):
        pick = onehot(kind_ref[...], i * 128, 128)
        start = pl.multiple_of((i // 9) * H_CORE + (i % 9) * D, 16)
        relbuf[pl.ds(start, D)] = dot(summand[...], pick, NT).astype(BF16)
        return carry

    def core_copy():
        other = pl.ds(pl.multiple_of((1 - c) * H_CORE, H_CORE), H_CORE)
        return remote(relbuf.at[other], core_recv, co_s.at[0], co_r.at[0], dev_c)

    lax.fori_loop(0, 18, relation_part, 0)
    core_copy().start()

    def c_copy(j, gi):
        return remote(
            csend.at[j, gi], crecv.at[NX - j, gi], cs_s.at[j, gi], cs_r.at[NX - j, gi], dev_x(j)
        )

    def spread(j, gi):
        pick = onehot(place_ref[...], (j * 8 + gi) * SLOTS, SLOTS)
        return dot(dtarget[...], pick, NT).astype(BF16)

    def send_group(gi):
        def body(j, carry):
            csend[j, gi] = spread(j, gi)
            c_copy(j, gi).start()
            return carry

        lax.fori_loop(1, NX, body, 0)
        crecv[0, gi] = spread(0, gi)

    def dneg_copy(k):
        return remote(dneg, dnegpart.at[NX - k], dn_s.at[k], dn_r.at[NX - k], dev_x(k))

    for k in range(1, NX):
        dneg_copy(k).start()
    send_group(2)

    core_copy().wait_recv()
    own = pl.ds(pl.multiple_of(c * H_CORE, H_CORE), H_CORE)
    relbuf[own] = (relbuf[own].astype(F32) + core_recv[...].astype(F32)).astype(BF16)

    def rel_rows(cc, yy, xx, zz, n):
        return pl.ds(pl.multiple_of(cc * H_CORE + yy * H_Y + xx * H_X + zz * H_Z, 32), n)

    def ry_copy(k):
        rows = rel_rows(c, lax.rem(y + k, NY), 0, 0, H_Y)
        return remote(relbuf.at[rows], y_recv.at[NY - k], ry_s.at[0, k], ry_r.at[0, NY - k], dev_y(k))

    for k in range(1, NY):
        ry_copy(k).start()

    send_group(1)
    send_group(0)

    pick_src = onehot(srow_ref[...], 0, R)
    src_grad = dot(dsource[...], pick_src, NT)
    new_table, new_state = adagrad(first_ref[...], fstate_ref[...], src_grad)
    first_new[...] = new_table
    fstate_new[...] = new_state

    for k in range(1, NX):
        remote(dneg, dnegpart.at[k], dn_s.at[k], dn_r.at[k], dev_x(k)).wait_recv()
    neg_sum = dneg[...].astype(F32)
    for k in range(1, NX):
        neg_sum = neg_sum + dnegpart[k].astype(F32)
    dnegpart[0] = neg_sum.astype(BF16)

    def wait_c(gi):
        for k in range(1, NX):
            remote(csend.at[k, gi], crecv.at[k, gi], cs_s.at[k, gi], cs_r.at[k, gi], dev_x(k)).wait_recv()

    def line_sum(gi, li):
        offset = GROUPS[gi][li]
        total = dot(dnegpart[0], onehot(negs, lax.rem(z + offset, NZ) * R, R), NT)
        for k in range(NX):
            total = total + dot(crecv[k, gi], onehot(asked[k][gi : gi + 1, :], li * R, R), NT)
        return total

    def ring_copy(way, s, q):
        send, recv = (up_send, up_recv) if way == 0 else (down_send, down_recv)
        rows = pl.ds(*CUTS[q])
        return remote(
            send.at[s, rows], recv.at[s, rows], rs_s.at[way, s, q], rs_r.at[way, s, q],
            dev_z(1 if way == 0 else NZ - 1),
        )

    def ring_cuts(way, s):
        return range(4) if s > 0 else ((0, 1) if way == 0 else (2, 3))

    def ring_step(way, s, total):
        send, recv = (up_send, up_recv) if way == 0 else (down_send, down_recv)
        for q in range(4):
            at, size = CUTS[q]
            rows = slice(at, at + size)
            part = total[rows]
            if s > 0 and q in ring_cuts(way, s - 1):
                ring_copy(way, s - 1, q).wait_recv()
                part = part + recv[s - 1, rows].astype(F32)
            if q in ring_cuts(way, s):
                send[s, rows] = part.astype(BF16)
                ring_copy(way, s, q).start()

    wait_c(2)
    total = line_sum(2, 2)
    ring_step(0, 0, total)
    ring_step(1, 0, total)
    ring_step(0, 1, line_sum(2, 0))
    ring_step(1, 1, line_sum(2, 1))

    def wait_y():
        for k in range(1, NY):
            remote(y_recv.at[k], y_recv.at[k], ry_s.at[0, k], ry_r.at[0, k], dev_y(k)).wait_recv()

    wait_y()
    total = relbuf[rel_rows(c, y, 0, 0, H_Y)].astype(F32)
    for k in range(1, NY):
        total = total + y_recv[k].astype(F32)
    red_y[...] = total.astype(BF16)

    def rx_copy(k):
        rows = pl.ds(pl.multiple_of(lax.rem(x + k, NX) * H_X, H_X), H_X)
        return remote(red_y.at[rows], x_recv.at[NX - k], rx_s.at[0, k], rx_r.at[0, NX - k], dev_x(k))

    for k in range(1, NX):
        rx_copy(k).start()

    wait_c(1)
    ring_step(0, 2, line_sum(1, 0))
    ring_step(1, 2, line_sum(1, 1))

    for k in range(1, NX):
        remote(x_recv.at[k], x_recv.at[k], rx_s.at[0, k], rx_r.at[0, k], dev_x(k)).wait_recv()
    total = red_y[pl.ds(pl.multiple_of(x * H_X, H_X), H_X)].astype(F32)
    for k in range(1, NX):
        total = total + x_recv[k].astype(F32)
    red_x[...] = total.astype(BF16)

    def rz_copy(k):
        rows = pl.ds(pl.multiple_of(lax.rem(z + k, NZ) * H_Z, H_Z), H_Z)
        return remote(red_x.at[rows], z_recv.at[NZ - k], rz_s.at[0, k], rz_r.at[0, NZ - k], dev_z(k))

    for k in range(1, NZ):
        rz_copy(k).start()

    wait_c(0)
    near = line_sum(0, 1)
    for k in range(1, NZ):
        remote(z_recv.at[k], z_recv.at[k], rz_s.at[0, k], rz_r.at[0, k], dev_z(k)).wait_recv()
    total = red_x[pl.ds(pl.multiple_of(z * H_Z, H_Z), H_Z)].astype(F32)
    for k in range(1, NZ):
        total = total + z_recv[k].astype(F32)
    mine_rows = rel_rows(c, y, x, z, H_Z)
    rel_out[mine_rows] = total.astype(BF16)

    def back_copy(rows, ss, rs, dev):
        return remote(rel_out.at[rows], rel_out.at[rows], ss, rs, dev)

    for k in range(1, NZ):
        back_copy(mine_rows, rz_s.at[1, k], rz_r.at[1, NZ - k], dev_z(k)).start()

    ring_step(0, 3, near)
    ring_step(1, 3, line_sum(0, 2))

    for k in range(1, NZ):
        rows = rel_rows(c, y, x, lax.rem(z + k, NZ), H_Z)
        back_copy(rows, rz_s.at[1, k], rz_r.at[1, k], dev_z(k)).wait_recv()
    x_rows = rel_rows(c, y, x, 0, H_X)
    for k in range(1, NX):
        back_copy(x_rows, rx_s.at[1, k], rx_r.at[1, NX - k], dev_x(k)).start()
    total = line_sum(0, 0)
    for k in range(1, NX):
        rows = rel_rows(c, y, lax.rem(x + k, NX), 0, H_X)
        back_copy(rows, rx_s.at[1, k], rx_r.at[1, k], dev_x(k)).wait_recv()
    y_rows = rel_rows(c, y, 0, 0, H_Y)
    for k in range(1, NY):
        back_copy(y_rows, ry_s.at[1, k], ry_r.at[1, NY - k], dev_y(k)).start()

    for q in range(4):
        for way in (0, 1):
            ring_copy(way, 3, q).wait_recv()
    total = total + up_recv[3].astype(F32) + down_recv[3].astype(F32)
    new_table, new_state = adagrad(second_ref[...], sstate_ref[...], total)
    second_new[...] = new_table
    sstate_new[...] = new_state

    for k in range(1, NY):
        rows = rel_rows(c, lax.rem(y + k, NY), 0, 0, H_Y)
        back_copy(rows, ry_s.at[1, k], ry_r.at[1, k], dev_y(k)).wait_recv()
    c_rows = rel_rows(c, 0, 0, 0, H_CORE)
    last = back_copy(c_rows, co_s.at[1], co_r.at[1], dev_c)
    last.start()
    rows = rel_rows(1 - c, 0, 0, 0, H_CORE)
    back_copy(rows, co_s.at[1], co_r.at[1], dev_c).wait_recv()

    for way in (0, 1):
        for s in range(4):
            for q in gather_cuts(way, s):
                gather_copy(way, s, q).wait_send()
            for q in ring_cuts(way, s):
                ring_copy(way, s, q).wait_send()
    for k in range(1, NX):
        req_copy(k).wait_send()
        neg_copy(k).wait_send()
        dneg_copy(k).wait_send()
        rx_copy(k).wait_send()
        back_copy(x_rows, rx_s.at[1, k], rx_r.at[1, k], dev_x(k)).wait_send()
        for gi in range(3):
            serve_copy(k, gi).wait_send()
            c_copy(k, gi).wait_send()
    for k in range(1, NY):
        ry_copy(k).wait_send()
        back_copy(y_rows, ry_s.at[1, k], ry_r.at[1, k], dev_y(k)).wait_send()
    for k in range(1, NZ):
        rz_copy(k).wait_send()
        back_copy(mine_rows, rz_s.at[1, k], rz_r.at[1, k], dev_z(k)).wait_send()
    core_copy().wait_send()
    last.wait_send()


def step_call(*args):
    vmem = pl.BlockSpec(memory_space=pltpu.VMEM)
    dma = pltpu.SemaphoreType.DMA
    return pl.pallas_call(
        step_kernel,
        out_shape=(
            jax.ShapeDtypeStruct((D, R), F32),
            jax.ShapeDtypeStruct((1, R), F32),
            jax.ShapeDtypeStruct((D, R), F32),
            jax.ShapeDtypeStruct((1, R), F32),
            jax.ShapeDtypeStruct((2 * H_CORE, 128), BF16),
        ),
        in_specs=[vmem] * len(args),
        out_specs=(vmem,) * 5,
        scratch_shapes=[
            pltpu.VMEM((NZ, D, R), BF16),
            pltpu.VMEM((NX, 8, SLOTS), jnp.int32),
            pltpu.VMEM((NX, 8, SLOTS), jnp.int32),
            pltpu.VMEM((NX, 3, D, SLOTS), BF16),
            pltpu.VMEM((NX, 3, D, SLOTS), BF16),
            pltpu.VMEM((NX, D, 2 * NL), BF16),
            pltpu.VMEM((1, E), jnp.int32),
            pltpu.VMEM((3, D, K), BF16),
            pltpu.VMEM((D, E), F32),
            pltpu.VMEM((D, E), BF16),
            pltpu.VMEM((D, E), BF16),
            pltpu.VMEM((D, E), BF16),
            pltpu.VMEM((D, E), BF16),
            pltpu.VMEM((D, E), BF16),
            pltpu.VMEM((D, E), BF16),
            pltpu.VMEM((D, 2 * NL), BF16),
            pltpu.VMEM((NX, D, 2 * NL), BF16),
            pltpu.VMEM((NX, 3, D, SLOTS), BF16),
            pltpu.VMEM((NX, 3, D, SLOTS), BF16),
            pltpu.VMEM((4, D, R), BF16),
            pltpu.VMEM((4, D, R), BF16),
            pltpu.VMEM((4, D, R), BF16),
            pltpu.VMEM((4, D, R), BF16),
            pltpu.VMEM((2 * H_CORE, 128), BF16),
            pltpu.VMEM((H_CORE, 128), BF16),
            pltpu.VMEM((NY, H_Y, 128), BF16),
            pltpu.VMEM((NX, H_X, 128), BF16),
            pltpu.VMEM((NZ, H_Z, 128), BF16),
            pltpu.VMEM((H_Y, 128), BF16),
            pltpu.VMEM((H_X, 128), BF16),
            dma((2, 4, 4)), dma((2, 4, 4)),
            dma((NX,)), dma((NX,)),
            dma((NX, 3)), dma((NX, 3)),
            dma((NX,)), dma((NX,)),
            dma((NX, 3)), dma((NX, 3)),
            dma((NX,)), dma((NX,)),
            dma((2, 4, 4)), dma((2, 4, 4)),
            dma((2,)), dma((2,)),
            dma((2, NY)), dma((2, NY)),
            dma((2, NX)), dma((2, NX)),
            dma((2, NZ)), dma((2, NZ)),
        ],
        compiler_params=pltpu.CompilerParams(
            collective_id=0, has_side_effects=True, vmem_limit_bytes=60 * 1024 * 1024
        ),
        name="edge_step",
    )(*args)


def relation_kernel(grad_ref, diag_ref, state_ref, diag_new, state_new):
    i = pl.program_id(0)
    for j in range(2):
        tile = 2 * i + j
        start = pl.multiple_of((tile // 9) * H_CORE + (tile % 9) * D, 16)
        lanes = slice(j * 128, (j + 1) * 128)
        new, state = adagrad(diag_ref[:, lanes], state_ref[:, lanes], grad_ref[pl.ds(start, D)].astype(F32))
        diag_new[:, lanes] = new
        state_new[:, lanes] = state


def relation_call(grad, diag, state):
    lanes = lambda rows: pl.BlockSpec((rows, 256), lambda i: (0, i))
    return pl.pallas_call(
        relation_kernel,
        grid=(K // 256,),
        out_shape=(jax.ShapeDtypeStruct((D, K), F32), jax.ShapeDtypeStruct((1, K), F32)),
        in_specs=[pl.BlockSpec((2 * H_CORE, 128), lambda i: (0, 0)), lanes(D), lanes(1)],
        out_specs=(lanes(D), lanes(1)),
        compiler_params=pltpu.CompilerParams(vmem_limit_bytes=40 * 1024 * 1024),
        name="relation_update",
    )(grad, diag, state)


def on_device(
    first_table, first_state, second_table, second_state, relation_diag, relation_state,
    source_row, target_owner, target_row, relation_id, negative_id,
):
    diag = relation_diag.T
    negs = jnp.pad(negative_id[0], ((0, 0), (0, NL - NEG)), constant_values=-(1 << 20)).reshape(1, 2 * NL)
    first_new, first_state_new, second_new, second_state_new, rel_grad = step_call(
        first_table[0].T, first_state, second_table[0].T, second_state, diag,
        source_row, target_owner.reshape(1, E), target_row, relation_id, negs,
    )
    diag_new, state_new = relation_call(rel_grad, diag, relation_state.reshape(1, K))
    return (
        first_new.T[None], first_state_new, second_new.T[None], second_state_new,
        diag_new.T, state_new.reshape(K),
    )


def solution(mesh):
    in_specs = (
        P("group", "owner", None),
        P("group", "owner"),
        P("group", "owner", None),
        P("group", "owner"),
        P(),
        P(),
        P("group", "owner"),
        P("group", "owner", None),
        P("group", "owner"),
        P("group", "owner"),
        P("group", None, None),
    )
    out_specs = (
        P("group", "owner", None),
        P("group", "owner"),
        P("group", "owner", None),
        P("group", "owner"),
        P(),
        P(),
    )
    return jax.shard_map(
        on_device, mesh=mesh, in_specs=in_specs, out_specs=out_specs, check_vma=False
    )
```

```python
import jax
import jax.numpy as jnp
from jax import lax
from jax.experimental import pallas as pl
from jax.experimental.pallas import tpu as pltpu
from jax.sharding import PartitionSpec as P

MESH = pl.DeviceIdType.MESH
F32 = jnp.float32
BF16 = jnp.bfloat16
LEARN = 0.1

D = 400
R = 512
E = 1024
BLOCK = 512
NEG = 100
NL = 128
K = 2304
NX, NY, NZ = 4, 4, 8
SLOTS = 256

GROUPS = ((7, 0, 1), (2, 6), (3, 4, 5))
SPOT = (1, 2, 3, 5, 6, 7, 4, 0)
CUTS = ((0, 96), (96, 112), (208, 96), (304, 96))
UP = (0, 7, 6, 5, 4)
DOWN = (0, 1, 2, 3, 4)
HALF = 208

H_CORE, H_PART, H_Y, H_X, H_Z = 4096, 2048, 512, 128, 16
Y_ROWS = (512, 400)
NEG_X, NEG_Z = 128, 16
NEG_ROWS = 512


def tile_rows(half, i):
    return half * H_CORE + (i * D if i < 5 else H_PART + (i - 5) * H_Y)


NN = (((1,), (0,)), ((), ()))
NT = (((1,), (1,)), ((), ()))
TN = (((0,), (0,)), ((), ()))


def dot(a, b, dims):
    return lax.dot_general(a, b, dims, preferred_element_type=F32)


def onehot(vec, base, n):
    rows = lax.broadcasted_iota(jnp.int32, (n, vec.shape[1]), 0)
    return jnp.where(rows == vec - base, 1.0, 0.0).astype(BF16)


def adagrad(table, state, grad):
    state_new = state + jnp.sum(grad * grad, axis=0, keepdims=True) * (1.0 / D)
    return table - LEARN * grad * (1.0 / jnp.sqrt(state_new)), state_new


def step_kernel(
    first_hbm, second_ref, diag_hbm, srow_ref, towner_ref, trow_ref, kind_ref, neg_ref,
    first_grad, second_grad, rel_out,
    first_ref, diag_ref, tabs, req, asked, serve, back, place_ref, neg_ids,
    splits, relrow, srcrow, query, dst, summand, dsource, dtarget, early,
    csend, crecv, up_send, up_recv, down_send, down_recv, lsum,
    neg_src, neg_xr, neg_xs, neg_zr, neg_out,
    relbuf, core_recv, y_recv, x_recv, z_recv, red_y, red_x,
    dg_s, ag_s, ag_r, rq_s, rq_r, sv_s, sv_r, cs_s, cs_r, rs_s, rs_r, nx_s, nx_r, nz_s, nz_r,
    co_s, co_r, ry_s, ry_r, rx_s, rx_r, rz_s, rz_r,
):
    g = lax.axis_index("group")
    o = lax.axis_index("owner")
    x, z = o // NZ, o % NZ
    y, c = g // 2, g % 2

    def dev_x(k):
        return (g, lax.rem(x + k, NX) * NZ + z)

    def dev_z(k):
        return (g, x * NZ + lax.rem(z + k, NZ))

    def dev_y(k):
        return (lax.rem(y + k, NY) * 2 + c, o)

    dev_c = (y * 2 + 1 - c, o)

    barrier = pltpu.get_barrier_semaphore()
    for peer in [dev_x(k) for k in range(1, NX)] + [dev_z(k) for k in range(1, NZ)] + [
        dev_y(k) for k in range(1, NY)
    ] + [dev_c]:
        pl.semaphore_signal(barrier, inc=1, device_id=peer, device_id_type=MESH)
    load_diag = pltpu.make_async_copy(diag_hbm, diag_ref, dg_s.at[0])
    load_first = pltpu.make_async_copy(first_hbm, first_ref, dg_s.at[1])
    load_first.start()
    load_diag.start()
    def table_lanes(offset):
        return pl.ds(SPOT[offset] * R, R)

    tabs[:, table_lanes(0)] = second_ref[...].astype(BF16)
    pl.semaphore_wait(barrier, NX + NZ + NY - 3 + 1)

    def remote(src, dst_, ss, rs, dev):
        return pltpu.make_async_remote_copy(
            src_ref=src, dst_ref=dst_, send_sem=ss, recv_sem=rs, device_id=dev, device_id_type=MESH
        )

    def gather_copy(way, step, q):
        path = UP if way == 0 else DOWN
        rows = pl.ds(*CUTS[q])
        return remote(
            tabs.at[rows, table_lanes(path[step])], tabs.at[rows, table_lanes(path[step + 1])],
            ag_s.at[way, step, q], ag_r.at[way, step, q], dev_z(1 if way == 0 else NZ - 1),
        )

    def gather_cuts(way, step):
        return range(4) if step < 3 else ((0, 1) if way == 0 else (2, 3))

    for q in range(4):
        for way in (0, 1):
            gather_copy(way, 0, q).start()

    def forward(step):
        for q in range(4):
            for way in (0, 1):
                if q in gather_cuts(way, step):
                    gather_copy(way, step, q).wait_recv()
                    if step < 3 and q in gather_cuts(way, step + 1):
                        gather_copy(way, step + 1, q).start()

    towner, trow = towner_ref[...], trow_ref[...]
    far = lax.rem(towner % NZ - z + NZ, NZ)
    side = lax.rem(towner // NZ - x + NX, NX)
    group = jnp.zeros_like(far)
    local = jnp.zeros_like(far)
    for gi, members in enumerate(GROUPS):
        for li, offset in enumerate(members):
            group = jnp.where(far == offset, gi, group)
            local = jnp.where(far == offset, li, local)
    kind_of = side * 8 + group
    mine = jnp.where(lax.broadcasted_iota(jnp.int32, (32, E), 0) == kind_of, 1.0, 0.0)
    before_mask = jnp.where(
        lax.broadcasted_iota(jnp.int32, (E, E), 0) < lax.broadcasted_iota(jnp.int32, (E, E), 1), 1.0, 0.0
    ).astype(BF16)
    before = dot(mine.astype(BF16), before_mask, NN)
    slot = jnp.sum(mine * before, axis=0, keepdims=True).astype(jnp.int32)
    for gi in range(3):
        place_ref[gi : gi + 1, :] = jnp.where(group == gi, side * SLOTS + slot, -1)
    value = local * R + trow + 1
    high = (value // 16).astype(F32)
    low = (value % 16).astype(F32)
    sends = jnp.concatenate([mine * high, mine * low], axis=0).astype(BF16)
    found = dot(sends, onehot(slot, 0, SLOTS), NT)
    wanted = (found[0:32] * 16.0 + found[32:64]).astype(jnp.int32) - 1
    asked[:, 0:SLOTS] = wanted[0:8]
    for k in range(1, NX):
        req[k] = wanted[8 * k : 8 * k + 8]

    def req_copy(k):
        return remote(req.at[k], asked.at[:, pl.ds((NX - k) * SLOTS, SLOTS)], rq_s.at[k], rq_r.at[NX - k], dev_x(k))

    for k in range(1, NX):
        req_copy(k).start()

    def neg_x_copy(u, k):
        rows = pl.ds(pl.multiple_of(lax.rem(x + k, NX) * NEG_X, NEG_X), NEG_X)
        return remote(neg_src.at[u, rows], neg_xr.at[u, NX - k], nx_s.at[u, 0, k], nx_r.at[u, 0, NX - k], dev_x(k))

    def neg_z_copy(u, k):
        rows = pl.ds(pl.multiple_of(lax.rem(z + k, NZ) * NEG_Z, NEG_Z), NEG_Z)
        return remote(neg_xs.at[u, rows], neg_zr.at[u, NZ - k], nz_s.at[u, 0, k], nz_r.at[u, 0, NZ - k], dev_z(k))

    def neg_zb_copy(u, k, way):
        at = lax.rem(z + k, NZ) if way else z
        rows = pl.ds(pl.multiple_of(x * NEG_X + at * NEG_Z, NEG_Z), NEG_Z)
        i = k if way else NZ - k
        return remote(neg_out.at[u, rows], neg_out.at[u, rows], nz_s.at[u, 1, k], nz_r.at[u, 1, i], dev_z(k))

    def neg_xb_copy(u, k, way):
        at = lax.rem(x + k, NX) if way else x
        rows = pl.ds(pl.multiple_of(at * NEG_X, NEG_X), NEG_X)
        i = k if way else NX - k
        return remote(neg_out.at[u, rows], neg_out.at[u, rows], nx_s.at[u, 1, k], nx_r.at[u, 1, i], dev_x(k))

    def neg_start(u):
        for k in range(1, NX):
            neg_x_copy(u, k).start()

    def neg_second(u):
        for k in range(1, NX):
            remote(neg_xr.at[u, k], neg_xr.at[u, k], nx_s.at[u, 0, k], nx_r.at[u, 0, k], dev_x(k)).wait_recv()
        total = neg_src[u, pl.ds(pl.multiple_of(x * NEG_X, NEG_X), NEG_X)].astype(F32)
        for k in range(1, NX):
            total = total + neg_xr[u, k].astype(F32)
        neg_xs[u] = total.astype(BF16)
        for k in range(1, NZ):
            neg_z_copy(u, k).start()

    def neg_third(u):
        for k in range(1, NZ):
            remote(neg_zr.at[u, k], neg_zr.at[u, k], nz_s.at[u, 0, k], nz_r.at[u, 0, k], dev_z(k)).wait_recv()
        total = neg_xs[u, pl.ds(pl.multiple_of(z * NEG_Z, NEG_Z), NEG_Z)].astype(F32)
        for k in range(1, NZ):
            total = total + neg_zr[u, k].astype(F32)
        neg_out[u, pl.ds(pl.multiple_of(x * NEG_X + z * NEG_Z, NEG_Z), NEG_Z)] = total.astype(BF16)
        for k in range(1, NZ):
            neg_zb_copy(u, k, 0).start()

    def neg_fourth(u):
        for k in range(1, NZ):
            neg_zb_copy(u, k, 1).wait_recv()
        for k in range(1, NX):
            neg_xb_copy(u, k, 0).start()

    def neg_last(u):
        for k in range(1, NX):
            neg_xb_copy(u, k, 1).wait_recv()

    neg_ids[...] = jnp.full((1, 2 * NL), -(1 << 20), jnp.int32)
    for b in range(2):
        neg_ids[:, b * NL : b * NL + NEG] = neg_ref[b : b + 1, :]
    negs = neg_ids[...] - o * R
    neg_src[0, 0:D] = dot(tabs[:, table_lanes(0)], onehot(negs, 0, R), NN).astype(BF16)
    for u in range(2):
        neg_src[u, D:NEG_ROWS] = jnp.zeros((NEG_ROWS - D, 2 * NL), BF16)
    neg_start(0)

    load_first.wait()
    first_copy = first_ref[...].astype(BF16)
    for b in range(2):
        lanes = slice(b * BLOCK, (b + 1) * BLOCK)
        srcrow[:, lanes] = dot(first_copy, onehot(srow_ref[:, lanes], 0, R), NN).astype(BF16)

    for k in range(1, NX):
        remote(req.at[k], asked.at[:, pl.ds(k * SLOTS, SLOTS)], rq_s.at[k], rq_r.at[k], dev_x(k)).wait_recv()

    def lanes_of(j):
        start = j * SLOTS
        return pl.ds(start if isinstance(j, int) else pl.multiple_of(start, SLOTS), SLOTS)

    def serve_copy(j, gi):
        return remote(
            serve.at[j, gi], back.at[gi, :, lanes_of(NX - j)], sv_s.at[j, gi], sv_r.at[NX - j, gi], dev_x(j)
        )

    def serve_rows(j, gi):
        members = GROUPS[gi]
        start = SPOT[members[0]] * R
        rows = len(members) * R
        want = asked[gi : gi + 1, lanes_of(j)]
        return dot(tabs[:, start : start + rows], onehot(want, 0, rows), NN).astype(BF16)

    def serve_group(gi):
        def body(j, carry):
            serve[j, gi] = serve_rows(j, gi)
            serve_copy(j, gi).start()
            return carry

        lax.fori_loop(1, NX, body, 0)

    def serve_own(gi):
        back[gi, :, 0:SLOTS] = serve_rows(0, gi)

    def relation_rows(n):
        def body(i, carry):
            lanes = pl.ds(pl.multiple_of(i * 256, 256), 256)
            pick = onehot(kind_ref[:, lanes], 0, K)
            relrow[:, lanes] = (
                dot(splits[0], pick, NN) + dot(splits[1], pick, NN) + dot(splits[2], pick, NN)
            )
            return carry

        lax.fori_loop(n, n + 1, body, 0)

    def wait_back(gi):
        for k in range(1, NX):
            remote(
                serve.at[k, gi], back.at[gi, :, lanes_of(k)], sv_s.at[k, gi], sv_r.at[k, gi], dev_x(k)
            ).wait_recv()

    def collect(gi, first):
        def body(b, carry):
            lanes = pl.ds(pl.multiple_of(b * 256, 256), 256)
            pick = onehot(place_ref[gi : gi + 1, lanes], 0, NX * SLOTS)
            rows = dot(back[gi], pick, NN).astype(BF16)
            dst[:, lanes] = rows if first else dst[:, lanes] + rows
            return carry

        lax.fori_loop(0, E // 256, body, 0)

    forward(0)
    serve_group(0)
    neg_second(0)
    serve_own(0)
    load_diag.wait()
    diag = diag_ref[...]
    high_part = diag.astype(BF16)
    rest = diag - high_part.astype(F32)
    splits[0] = high_part
    splits[1] = rest.astype(BF16)
    splits[2] = (rest - splits[1].astype(F32)).astype(BF16)
    forward(1)
    serve_group(1)
    neg_third(0)
    serve_own(1)
    relation_rows(0)
    forward(2)
    neg_fourth(0)
    relation_rows(1)
    forward(3)
    serve_group(2)
    serve_own(2)
    relation_rows(2)
    relation_rows(3)
    query[...] = (srcrow[...].astype(F32) * relrow[...]).astype(BF16)
    neg_last(0)

    scale = 1.0 / (BLOCK - 1 + NEG)
    for b in range(2):
        lanes = slice(b * BLOCK, (b + 1) * BLOCK)
        nl = slice(b * NL, (b + 1) * NL)
        q, n = query[:, lanes], neg_out[0, 0:D, nl]
        d_sampled = (scale * jax.nn.sigmoid(dot(q, n, TN))).astype(BF16)
        early[:, lanes] = dot(n, d_sampled, NT)
        neg_src[1, 0:D, nl] = dot(q, d_sampled, NN).astype(BF16)
    wait_back(0)
    collect(0, True)
    wait_back(1)
    collect(1, False)
    for half in range(2):
        at = half * H_CORE
        relbuf[at + 2000 : at + H_PART] = jnp.zeros((H_PART - 2000, 128), BF16)
        for i in range(4):
            gap = at + H_PART + i * H_Y + D
            relbuf[gap : gap + H_Y - D] = jnp.zeros((H_Y - D, 128), BF16)
    red_y[1, D:H_Y] = jnp.zeros((H_Y - D, 128), BF16)
    wait_back(2)
    collect(2, False)

    diagonal = lax.broadcasted_iota(jnp.int32, (BLOCK, BLOCK), 0) == lax.broadcasted_iota(
        jnp.int32, (BLOCK, BLOCK), 1
    )
    for b in range(2):
        lanes = slice(b * BLOCK, (b + 1) * BLOCK)
        q, t = query[:, lanes], dst[:, lanes]
        batch = dot(q, t, TN)
        d_batch = (
            jax.nn.sigmoid(jnp.where(diagonal, -batch, batch)) * jnp.where(diagonal, -1.0, scale)
        ).astype(BF16)
        d_query = dot(t, d_batch, NT) + early[:, lanes]
        dsource[:, lanes] = (d_query * relrow[:, lanes]).astype(BF16)
        summand[:, lanes] = (d_query * srcrow[:, lanes].astype(F32)).astype(BF16)
        dtarget[:, lanes] = dot(q, d_batch, NN).astype(BF16)

    def relation_pair(i):
        pick = onehot(kind_ref[...], i * 256, 256)
        pair = dot(summand[...], pick, NT).astype(BF16)
        for half in range(2):
            at = tile_rows(half, i)
            relbuf[at : at + D] = pair[:, half * 128 : half * 128 + 128]

    def rel_rows(cc, p, yy, xx, zz, n):
        at = cc * H_CORE + p * H_PART + yy * H_Y + xx * H_X + zz * H_Z
        return pl.ds(pl.multiple_of(at, 16), n)

    def core_copy(p):
        return remote(relbuf.at[rel_rows(1 - c, p, 0, 0, 0, H_PART)], core_recv.at[p], co_s.at[0, p], co_r.at[0, p], dev_c)

    def ry_copy(p, k):
        n = Y_ROWS[p]
        return remote(
            relbuf.at[rel_rows(c, p, lax.rem(y + k, NY), 0, 0, n)], y_recv.at[p, NY - k, pl.ds(0, n)],
            ry_s.at[0, p, k], ry_r.at[0, p, NY - k], dev_y(k),
        )

    def rx_copy(p, k):
        rows = pl.ds(pl.multiple_of(lax.rem(x + k, NX) * H_X, H_X), H_X)
        return remote(red_y.at[p, rows], x_recv.at[p, NX - k], rx_s.at[0, p, k], rx_r.at[0, p, NX - k], dev_x(k))

    def rz_copy(p, k):
        rows = pl.ds(pl.multiple_of(lax.rem(z + k, NZ) * H_Z, H_Z), H_Z)
        return remote(red_x.at[p, rows], z_recv.at[p, NZ - k], rz_s.at[0, p, k], rz_r.at[0, p, NZ - k], dev_z(k))

    def rzb_copy(p, k, way):
        rows = rel_rows(c, p, y, x, lax.rem(z + k, NZ) if way else z, H_Z)
        i = k if way else NZ - k
        return remote(rel_out.at[rows], rel_out.at[rows], rz_s.at[1, p, k], rz_r.at[1, p, i], dev_z(k))

    def rxb_copy(p, k, way):
        rows = rel_rows(c, p, y, lax.rem(x + k, NX) if way else x, 0, H_X)
        i = k if way else NX - k
        return remote(rel_out.at[rows], rel_out.at[rows], rx_s.at[1, p, k], rx_r.at[1, p, i], dev_x(k))

    def ryb_copy(p, k, way):
        rows = rel_rows(c, p, lax.rem(y + k, NY) if way else y, 0, 0, Y_ROWS[p])
        i = k if way else NY - k
        return remote(rel_out.at[rows], rel_out.at[rows], ry_s.at[1, p, k], ry_r.at[1, p, i], dev_y(k))

    def cb_copy(p, way):
        rows = rel_rows(1 - c if way else c, p, 0, 0, 0, H_PART)
        return remote(rel_out.at[rows], rel_out.at[rows], co_s.at[1, p], co_r.at[1, p], dev_c)

    def rel_y(p):
        remote(core_recv.at[p], core_recv.at[p], co_s.at[0, p], co_r.at[0, p], dev_c).wait_recv()
        own = rel_rows(c, p, 0, 0, 0, H_PART)
        relbuf[own] = (relbuf[own].astype(F32) + core_recv[p].astype(F32)).astype(BF16)
        for k in range(1, NY):
            ry_copy(p, k).start()

    def rel_x(p):
        n = Y_ROWS[p]
        for k in range(1, NY):
            part = y_recv.at[p, k, pl.ds(0, n)]
            remote(part, part, ry_s.at[0, p, k], ry_r.at[0, p, k], dev_y(k)).wait_recv()
        total = relbuf[rel_rows(c, p, y, 0, 0, n)].astype(F32)
        for k in range(1, NY):
            total = total + y_recv[p, k, 0:n].astype(F32)
        red_y[p, 0:n] = total.astype(BF16)
        for k in range(1, NX):
            rx_copy(p, k).start()

    def rel_z(p):
        for k in range(1, NX):
            remote(x_recv.at[p, k], x_recv.at[p, k], rx_s.at[0, p, k], rx_r.at[0, p, k], dev_x(k)).wait_recv()
        total = red_y[p, pl.ds(pl.multiple_of(x * H_X, H_X), H_X)].astype(F32)
        for k in range(1, NX):
            total = total + x_recv[p, k].astype(F32)
        red_x[p] = total.astype(BF16)
        for k in range(1, NZ):
            rz_copy(p, k).start()

    def rel_zb(p):
        for k in range(1, NZ):
            remote(z_recv.at[p, k], z_recv.at[p, k], rz_s.at[0, p, k], rz_r.at[0, p, k], dev_z(k)).wait_recv()
        total = red_x[p, pl.ds(pl.multiple_of(z * H_Z, H_Z), H_Z)].astype(F32)
        for k in range(1, NZ):
            total = total + z_recv[p, k].astype(F32)
        rel_out[rel_rows(c, p, y, x, z, H_Z)] = total.astype(BF16)
        for k in range(1, NZ):
            rzb_copy(p, k, 0).start()

    def rel_xb(p):
        for k in range(1, NZ):
            rzb_copy(p, k, 1).wait_recv()
        for k in range(1, NX):
            rxb_copy(p, k, 0).start()

    def rel_yb(p):
        for k in range(1, NX):
            rxb_copy(p, k, 1).wait_recv()
        for k in range(1, NY):
            ryb_copy(p, k, 0).start()

    def rel_cb(p):
        for k in range(1, NY):
            ryb_copy(p, k, 1).wait_recv()
        cb_copy(p, 0).start()

    def c_copy(j, gi):
        return remote(
            csend.at[j, gi], crecv.at[gi, :, lanes_of(NX - j)], cs_s.at[j, gi], cs_r.at[NX - j, gi], dev_x(j)
        )

    def spread(j, gi):
        pick = onehot(place_ref[gi : gi + 1, :], j * SLOTS, SLOTS)
        return dot(dtarget[...], pick, NT).astype(BF16)

    def send_group(gi):
        def body(j, carry):
            csend[j, gi] = spread(j, gi)
            c_copy(j, gi).start()
            return carry

        lax.fori_loop(1, NX, body, 0)

    def keep_group(gi):
        crecv[gi, :, 0:SLOTS] = spread(0, gi)

    def wait_c(gi):
        for k in range(1, NX):
            remote(
                csend.at[k, gi], crecv.at[gi, :, lanes_of(k)], cs_s.at[k, gi], cs_r.at[k, gi], dev_x(k)
            ).wait_recv()

    def line_sum(offset):
        gi = [offset in members for members in GROUPS].index(True)
        li = GROUPS[gi].index(offset)
        return dot(crecv[gi], onehot(asked[gi : gi + 1, :], li * R, R), NT)

    def ring_copy(way, s, q):
        send, recv = (up_send, up_recv) if way == 0 else (down_send, down_recv)
        rows = pl.ds(*CUTS[q])
        return remote(
            send.at[s, rows], recv.at[s, rows], rs_s.at[way, s, q], rs_r.at[way, s, q],
            dev_z(1 if way == 0 else NZ - 1),
        )

    def ring_cuts(way, s):
        return range(4) if s > 0 else ((0, 1) if way == 0 else (2, 3))

    def ring_part(s, turn):
        for i in range(2):
            for way in (0, 1):
                q = ((2, 3, 0, 1) if way == 0 else (0, 1, 2, 3))[2 * turn + i]
                if q not in ring_cuts(way, s):
                    continue
                send, recv = (up_send, up_recv) if way == 0 else (down_send, down_recv)
                at, size = CUTS[q]
                rows = slice(at, at + size)
                part = lsum[0 if s == 0 else way, rows]
                if s > 0 and q in ring_cuts(way, s - 1):
                    ring_copy(way, s - 1, q).wait_recv()
                    part = part + recv[s - 1, rows].astype(F32)
                send[s, rows] = part.astype(BF16)
                ring_copy(way, s, q).start()

    send_group(2)
    for i in range(5):
        relation_pair(i)
    core_copy(0).start()
    for i in range(5, 9):
        relation_pair(i)
    core_copy(1).start()
    rel_y(0)
    keep_group(2)
    rel_y(1)
    neg_start(1)
    first_grad[...] = dot(dsource[...], onehot(srow_ref[...], 0, R), NT)
    rel_x(0)
    wait_c(2)
    lsum[0] = line_sum(4)
    ring_part(0, 0)
    ring_part(0, 1)
    send_group(1)
    lsum[0] = line_sum(3)
    lsum[1] = line_sum(5)
    ring_part(1, 0)
    rel_z(0)
    rel_x(1)
    keep_group(1)
    ring_part(1, 1)
    neg_second(1)
    rel_zb(0)
    rel_z(1)
    send_group(0)
    wait_c(1)
    lsum[0] = line_sum(2)
    lsum[1] = line_sum(6)
    ring_part(2, 0)
    rel_xb(0)
    keep_group(0)
    rel_zb(1)
    ring_part(2, 1)
    neg_third(1)
    rel_yb(0)
    rel_xb(1)
    neg_fourth(1)
    wait_c(0)
    lsum[0] = line_sum(1)
    lsum[1] = line_sum(7)
    ring_part(3, 0)
    rel_yb(1)
    ring_part(3, 1)
    neg_last(1)
    total = line_sum(0) + dot(neg_out[1, 0:D], onehot(negs, 0, R), NT)
    rel_cb(0)

    for q in range(4):
        for way in (0, 1):
            ring_copy(way, 3, q).wait_recv()
    second_grad[...] = total + up_recv[3].astype(F32) + down_recv[3].astype(F32)
    rel_cb(1)
    cb_copy(0, 1).wait_recv()
    cb_copy(1, 1).wait_recv()

    for way in (0, 1):
        for s in range(4):
            for q in gather_cuts(way, s):
                gather_copy(way, s, q).wait_send()
            for q in ring_cuts(way, s):
                ring_copy(way, s, q).wait_send()
    for k in range(1, NX):
        req_copy(k).wait_send()
        for gi in range(3):
            serve_copy(k, gi).wait_send()
            c_copy(k, gi).wait_send()
    for u in range(2):
        for k in range(1, NX):
            neg_x_copy(u, k).wait_send()
            neg_xb_copy(u, k, 0).wait_send()
        for k in range(1, NZ):
            neg_z_copy(u, k).wait_send()
            neg_zb_copy(u, k, 0).wait_send()
    for p in range(2):
        core_copy(p).wait_send()
        cb_copy(p, 0).wait_send()
        for k in range(1, NY):
            ry_copy(p, k).wait_send()
            ryb_copy(p, k, 0).wait_send()
        for k in range(1, NX):
            rx_copy(p, k).wait_send()
            rxb_copy(p, k, 0).wait_send()
        for k in range(1, NZ):
            rz_copy(p, k).wait_send()
            rzb_copy(p, k, 0).wait_send()


def step_call(*args):
    vmem = pl.BlockSpec(memory_space=pltpu.VMEM)
    dma = pltpu.SemaphoreType.DMA
    return pl.pallas_call(
        step_kernel,
        out_shape=(
            jax.ShapeDtypeStruct((D, R), F32),
            jax.ShapeDtypeStruct((D, R), F32),
            jax.ShapeDtypeStruct((2 * H_CORE, 128), BF16),
        ),
        in_specs=[pl.BlockSpec(memory_space=pl.ANY) if i in (0, 2) else vmem for i in range(len(args))],
        out_specs=(vmem,) * 3,
        scratch_shapes=[
            pltpu.VMEM((D, R), F32),
            pltpu.VMEM((D, K), F32),
            pltpu.VMEM((D, NZ * R), BF16),
            pltpu.VMEM((NX, 8, SLOTS), jnp.int32),
            pltpu.VMEM((8, NX * SLOTS), jnp.int32),
            pltpu.VMEM((NX, 3, D, SLOTS), BF16),
            pltpu.VMEM((3, D, NX * SLOTS), BF16),
            pltpu.VMEM((8, E), jnp.int32),
            pltpu.VMEM((1, 2 * NL), jnp.int32),
            pltpu.VMEM((3, D, K), BF16),
            pltpu.VMEM((D, E), F32),
            pltpu.VMEM((D, E), BF16),
            pltpu.VMEM((D, E), BF16),
            pltpu.VMEM((D, E), BF16),
            pltpu.VMEM((D, E), BF16),
            pltpu.VMEM((D, E), BF16),
            pltpu.VMEM((D, E), BF16),
            pltpu.VMEM((D, E), F32),
            pltpu.VMEM((NX, 3, D, SLOTS), BF16),
            pltpu.VMEM((3, D, NX * SLOTS), BF16),
            pltpu.VMEM((4, D, R), BF16),
            pltpu.VMEM((4, D, R), BF16),
            pltpu.VMEM((4, D, R), BF16),
            pltpu.VMEM((4, D, R), BF16),
            pltpu.VMEM((2, D, R), F32),
            pltpu.VMEM((2, NEG_ROWS, 2 * NL), BF16),
            pltpu.VMEM((2, NX, NEG_X, 2 * NL), BF16),
            pltpu.VMEM((2, NEG_X, 2 * NL), BF16),
            pltpu.VMEM((2, NZ, NEG_Z, 2 * NL), BF16),
            pltpu.VMEM((2, NEG_ROWS, 2 * NL), BF16),
            pltpu.VMEM((2 * H_CORE, 128), BF16),
            pltpu.VMEM((2, H_PART, 128), BF16),
            pltpu.VMEM((2, NY, H_Y, 128), BF16),
            pltpu.VMEM((2, NX, H_X, 128), BF16),
            pltpu.VMEM((2, NZ, H_Z, 128), BF16),
            pltpu.VMEM((2, H_Y, 128), BF16),
            pltpu.VMEM((2, H_X, 128), BF16),
            dma((2,)),
            dma((2, 4, 4)), dma((2, 4, 4)),
            dma((NX,)), dma((NX,)),
            dma((NX, 3)), dma((NX, 3)),
            dma((NX, 3)), dma((NX, 3)),
            dma((2, 4, 4)), dma((2, 4, 4)),
            dma((2, 2, NX)), dma((2, 2, NX)),
            dma((2, 2, NZ)), dma((2, 2, NZ)),
            dma((2, 2)), dma((2, 2)),
            dma((2, 2, NY)), dma((2, 2, NY)),
            dma((2, 2, NX)), dma((2, 2, NX)),
            dma((2, 2, NZ)), dma((2, 2, NZ)),
        ],
        compiler_params=pltpu.CompilerParams(
            collective_id=0, has_side_effects=True, vmem_limit_bytes=60 * 1024 * 1024
        ),
        name="edge_step",
    )(*args)


def update_kernel(
    rel_grad, diag_ref, rstate_ref, first_ref, fstate_ref, first_grad, second_ref, sstate_ref, second_grad,
    diag_new, rstate_new, first_new, fstate_new, second_new, sstate_new,
):
    i = pl.program_id(0)
    for half in range(2):
        start = jnp.where(i < 5, i * D, H_PART + (i - 5) * H_Y) + half * H_CORE
        lanes = slice(half * 128, (half + 1) * 128)
        grad = rel_grad[pl.ds(pl.multiple_of(start, 16), D)].astype(F32)
        diag_new[:, lanes], rstate_new[:, lanes] = adagrad(diag_ref[:, lanes], rstate_ref[:, lanes], grad)

    @pl.when(i < 4)
    def _():
        first_new[...], fstate_new[...] = adagrad(first_ref[...], fstate_ref[...], first_grad[...])

    @pl.when(jnp.logical_and(i >= 4, i < 8))
    def _():
        second_new[...], sstate_new[...] = adagrad(second_ref[...], sstate_ref[...], second_grad[...])


def update_call(rel_grad, diag, rstate, first, fstate, first_grad, second, sstate, second_grad):
    pair = lambda rows: pl.BlockSpec((rows, 256), lambda i: (0, i))
    one = lambda rows: pl.BlockSpec((rows, 128), lambda i: (0, jnp.minimum(i, 3)))
    two = lambda rows: pl.BlockSpec((rows, 128), lambda i: (0, jnp.clip(i - 4, 0, 3)))
    shape = jax.ShapeDtypeStruct
    return pl.pallas_call(
        update_kernel,
        grid=(K // 256,),
        out_shape=(
            shape((D, K), F32), shape((1, K), F32), shape((D, R), F32), shape((1, R), F32),
            shape((D, R), F32), shape((1, R), F32),
        ),
        in_specs=[
            pl.BlockSpec((2 * H_CORE, 128), lambda i: (0, 0)),
            pair(D), pair(1), one(D), one(1), one(D), two(D), two(1), two(D),
        ],
        out_specs=(pair(D), pair(1), one(D), one(1), two(D), two(1)),
        compiler_params=pltpu.CompilerParams(vmem_limit_bytes=60 * 1024 * 1024),
        name="table_update",
    )(rel_grad, diag, rstate, first, fstate, first_grad, second, sstate, second_grad)


def on_device(
    first_table, first_state, second_table, second_state, relation_diag, relation_state,
    source_row, target_owner, target_row, relation_id, negative_id,
):
    diag, first, second = relation_diag.T, first_table[0].T, second_table[0].T
    first_grad, second_grad, rel_grad = step_call(
        first, second, diag,
        source_row, target_owner.reshape(1, E), target_row, relation_id, negative_id[0],
    )
    diag_new, state_new, first_new, first_state_new, second_new, second_state_new = update_call(
        rel_grad, diag, relation_state.reshape(1, K), first, first_state, first_grad, second, second_state, second_grad
    )
    return (
        first_new.T[None], first_state_new, second_new.T[None], second_state_new,
        diag_new.T, state_new.reshape(K),
    )


def solution(mesh):
    in_specs = (
        P("group", "owner", None),
        P("group", "owner"),
        P("group", "owner", None),
        P("group", "owner"),
        P(),
        P(),
        P("group", "owner"),
        P("group", "owner", None),
        P("group", "owner"),
        P("group", "owner"),
        P("group", None, None),
    )
    out_specs = (
        P("group", "owner", None),
        P("group", "owner"),
        P("group", "owner", None),
        P("group", "owner"),
        P(),
        P(),
    )
    return jax.shard_map(
        on_device, mesh=mesh, in_specs=in_specs, out_specs=out_specs, check_vma=False
    )
```

```python
import jax
import jax.numpy as jnp
from jax import lax
from jax.experimental import pallas as pl
from jax.experimental.pallas import tpu as pltpu
from jax.sharding import PartitionSpec as P

MESH = pl.DeviceIdType.MESH
F32 = jnp.float32
BF16 = jnp.bfloat16
LEARN = 0.1

D = 400
R = 512
E = 1024
BLOCK = 512
NEG = 100
NL = 128
K = 2304
NX, NY, NZ = 4, 4, 8
SLOTS = 256

GROUPS = ((7, 0, 1), (2, 6), (3, 4, 5))
SPOT = (1, 2, 3, 5, 6, 7, 4, 0)
CUTS = ((0, 96), (96, 112), (208, 96), (304, 96))
UP = (0, 7, 6, 5, 4)
DOWN = (0, 1, 2, 3, 4)
HALF = 208

H_CORE, H_PART, H_Y, H_X, H_Z = 4096, 2048, 512, 128, 16
Y_ROWS = (512, 400)
NEG_X, NEG_Z = 128, 16
NEG_ROWS = 512


def tile_rows(half, i):
    return half * H_CORE + (i * D if i < 5 else H_PART + (i - 5) * H_Y)


NN = (((1,), (0,)), ((), ()))
NT = (((1,), (1,)), ((), ()))
TN = (((0,), (0,)), ((), ()))


def dot(a, b, dims):
    return lax.dot_general(a, b, dims, preferred_element_type=F32)


def onehot(vec, base, n):
    rows = lax.broadcasted_iota(jnp.int32, (n, vec.shape[1]), 0)
    return jnp.where(rows == vec - base, 1.0, 0.0).astype(BF16)


def adagrad(table, state, grad):
    state_new = state + jnp.sum(grad * grad, axis=0, keepdims=True) * (1.0 / D)
    return table - LEARN * grad * (1.0 / jnp.sqrt(state_new)), state_new


def step_kernel(
    first_hbm, second_ref, diag_hbm, srow_ref, towner_ref, trow_ref, kind_ref, neg_ref,
    first_grad, second_grad, rel_out,
    first_ref, diag_ref, tabs, req, asked, serve, back, place_ref, neg_ids,
    splits, relrow, srcrow, query, query_t, dst, dsource, dtarget, early,
    crecv, up_send, up_recv, down_send, down_recv, lsum,
    neg_src, neg_xr, neg_xs, neg_zr, neg_out,
    relbuf, core_recv, y_recv, x_recv, z_recv, red_y, red_x,
    dg_s, ag_s, ag_r, rq_s, rq_r, sv_s, sv_r, cs_s, cs_r, rs_s, rs_r, nx_s, nx_r, nz_s, nz_r,
    co_s, co_r, ry_s, ry_r, rx_s, rx_r, rz_s, rz_r,
):
    g = lax.axis_index("group")
    o = lax.axis_index("owner")
    x, z = o // NZ, o % NZ
    y, c = g // 2, g % 2

    def dev_x(k):
        return (g, lax.rem(x + k, NX) * NZ + z)

    def dev_z(k):
        return (g, x * NZ + lax.rem(z + k, NZ))

    def dev_y(k):
        return (lax.rem(y + k, NY) * 2 + c, o)

    dev_c = (y * 2 + 1 - c, o)

    barrier = pltpu.get_barrier_semaphore()
    for peer in [dev_x(k) for k in range(1, NX)] + [dev_z(k) for k in range(1, NZ)] + [
        dev_y(k) for k in range(1, NY)
    ] + [dev_c]:
        pl.semaphore_signal(barrier, inc=1, device_id=peer, device_id_type=MESH)
    load_diag = pltpu.make_async_copy(diag_hbm, diag_ref, dg_s.at[0])
    load_first = pltpu.make_async_copy(first_hbm, first_ref, dg_s.at[1])
    load_first.start()
    load_diag.start()
    def table_lanes(offset):
        return pl.ds(SPOT[offset] * R, R)

    tabs[:, table_lanes(0)] = second_ref[...].astype(BF16)
    pl.semaphore_wait(barrier, NX + NZ + NY - 3 + 1)

    def remote(src, dst_, ss, rs, dev):
        return pltpu.make_async_remote_copy(
            src_ref=src, dst_ref=dst_, send_sem=ss, recv_sem=rs, device_id=dev, device_id_type=MESH
        )

    def gather_copy(way, step, q):
        path = UP if way == 0 else DOWN
        rows = pl.ds(*CUTS[q])
        return remote(
            tabs.at[rows, table_lanes(path[step])], tabs.at[rows, table_lanes(path[step + 1])],
            ag_s.at[way, step, q], ag_r.at[way, step, q], dev_z(1 if way == 0 else NZ - 1),
        )

    def gather_cuts(way, step):
        return range(4) if step < 3 else ((0, 1) if way == 0 else (2, 3))

    for q in range(4):
        for way in (0, 1):
            gather_copy(way, 0, q).start()

    def forward(step):
        for q in range(4):
            for way in (0, 1):
                if q in gather_cuts(way, step):
                    gather_copy(way, step, q).wait_recv()
                    if step < 3 and q in gather_cuts(way, step + 1):
                        gather_copy(way, step + 1, q).start()

    towner, trow = towner_ref[...], trow_ref[...]
    far = lax.rem(towner % NZ - z + NZ, NZ)
    side = lax.rem(towner // NZ - x + NX, NX)
    group = jnp.zeros_like(far)
    local = jnp.zeros_like(far)
    for gi, members in enumerate(GROUPS):
        for li, offset in enumerate(members):
            group = jnp.where(far == offset, gi, group)
            local = jnp.where(far == offset, li, local)
    kind_of = side * 8 + group
    mine = jnp.where(lax.broadcasted_iota(jnp.int32, (32, E), 0) == kind_of, 1.0, 0.0)
    before_mask = jnp.where(
        lax.broadcasted_iota(jnp.int32, (E, E), 0) < lax.broadcasted_iota(jnp.int32, (E, E), 1), 1.0, 0.0
    ).astype(BF16)
    before = dot(mine.astype(BF16), before_mask, NN)
    slot = jnp.sum(mine * before, axis=0, keepdims=True).astype(jnp.int32)
    for gi in range(3):
        place_ref[gi : gi + 1, :] = jnp.where(group == gi, side * SLOTS + slot, -1)
    value = local * R + trow + 1
    high = (value // 16).astype(F32)
    low = (value % 16).astype(F32)
    sends = jnp.concatenate([mine * high, mine * low], axis=0).astype(BF16)
    found = dot(sends, onehot(slot, 0, SLOTS), NT)
    wanted = (found[0:32] * 16.0 + found[32:64]).astype(jnp.int32) - 1
    asked[:, 0:SLOTS] = wanted[0:8]
    for k in range(1, NX):
        req[k] = wanted[8 * k : 8 * k + 8]

    def req_copy(k):
        return remote(req.at[k], asked.at[:, pl.ds((NX - k) * SLOTS, SLOTS)], rq_s.at[k], rq_r.at[NX - k], dev_x(k))

    for k in range(1, NX):
        req_copy(k).start()

    def neg_x_copy(u, k):
        rows = pl.ds(pl.multiple_of(lax.rem(x + k, NX) * NEG_X, NEG_X), NEG_X)
        return remote(neg_src.at[u, rows], neg_xr.at[u, NX - k], nx_s.at[u, 0, k], nx_r.at[u, 0, NX - k], dev_x(k))

    def neg_z_copy(u, k):
        rows = pl.ds(pl.multiple_of(lax.rem(z + k, NZ) * NEG_Z, NEG_Z), NEG_Z)
        return remote(neg_xs.at[u, rows], neg_zr.at[u, NZ - k], nz_s.at[u, 0, k], nz_r.at[u, 0, NZ - k], dev_z(k))

    def neg_zb_copy(u, k, way):
        at = lax.rem(z + k, NZ) if way else z
        rows = pl.ds(pl.multiple_of(x * NEG_X + at * NEG_Z, NEG_Z), NEG_Z)
        i = k if way else NZ - k
        return remote(neg_out.at[u, rows], neg_out.at[u, rows], nz_s.at[u, 1, k], nz_r.at[u, 1, i], dev_z(k))

    def neg_xb_copy(u, k, way):
        at = lax.rem(x + k, NX) if way else x
        rows = pl.ds(pl.multiple_of(at * NEG_X, NEG_X), NEG_X)
        i = k if way else NX - k
        return remote(neg_out.at[u, rows], neg_out.at[u, rows], nx_s.at[u, 1, k], nx_r.at[u, 1, i], dev_x(k))

    def neg_start(u):
        for k in range(1, NX):
            neg_x_copy(u, k).start()

    def neg_second(u):
        for k in range(1, NX):
            remote(neg_xr.at[u, k], neg_xr.at[u, k], nx_s.at[u, 0, k], nx_r.at[u, 0, k], dev_x(k)).wait_recv()
        total = neg_src[u, pl.ds(pl.multiple_of(x * NEG_X, NEG_X), NEG_X)].astype(F32)
        for k in range(1, NX):
            total = total + neg_xr[u, k].astype(F32)
        neg_xs[u] = total.astype(BF16)
        for k in range(1, NZ):
            neg_z_copy(u, k).start()

    def neg_third(u):
        for k in range(1, NZ):
            remote(neg_zr.at[u, k], neg_zr.at[u, k], nz_s.at[u, 0, k], nz_r.at[u, 0, k], dev_z(k)).wait_recv()
        total = neg_xs[u, pl.ds(pl.multiple_of(z * NEG_Z, NEG_Z), NEG_Z)].astype(F32)
        for k in range(1, NZ):
            total = total + neg_zr[u, k].astype(F32)
        neg_out[u, pl.ds(pl.multiple_of(x * NEG_X + z * NEG_Z, NEG_Z), NEG_Z)] = total.astype(BF16)
        for k in range(1, NZ):
            neg_zb_copy(u, k, 0).start()

    def neg_fourth(u):
        for k in range(1, NZ):
            neg_zb_copy(u, k, 1).wait_recv()
        for k in range(1, NX):
            neg_xb_copy(u, k, 0).start()

    def neg_last(u):
        for k in range(1, NX):
            neg_xb_copy(u, k, 1).wait_recv()

    neg_ids[...] = jnp.full((1, 2 * NL), -(1 << 20), jnp.int32)
    for b in range(2):
        neg_ids[:, b * NL : b * NL + NEG] = neg_ref[b : b + 1, :]
    negs = neg_ids[...] - o * R
    neg_src[0, 0:D] = dot(tabs[:, table_lanes(0)], onehot(negs, 0, R), NN).astype(BF16)
    for u in range(2):
        neg_src[u, D:NEG_ROWS] = jnp.zeros((NEG_ROWS - D, 2 * NL), BF16)
    neg_start(0)

    load_first.wait()
    first_copy = first_ref[...].astype(BF16)
    for b in range(2):
        lanes = slice(b * BLOCK, (b + 1) * BLOCK)
        srcrow[:, lanes] = dot(first_copy, onehot(srow_ref[:, lanes], 0, R), NN).astype(BF16)

    for k in range(1, NX):
        remote(req.at[k], asked.at[:, pl.ds(k * SLOTS, SLOTS)], rq_s.at[k], rq_r.at[k], dev_x(k)).wait_recv()

    def lanes_of(j):
        start = j * SLOTS
        return pl.ds(start if isinstance(j, int) else pl.multiple_of(start, SLOTS), SLOTS)

    def serve_copy(j, gi):
        return remote(
            serve.at[j, gi], back.at[gi, :, lanes_of(NX - j)], sv_s.at[j, gi], sv_r.at[NX - j, gi], dev_x(j)
        )

    def serve_rows(j, gi):
        members = GROUPS[gi]
        start = SPOT[members[0]] * R
        rows = len(members) * R
        want = asked[gi : gi + 1, lanes_of(j)]
        return dot(tabs[:, start : start + rows], onehot(want, 0, rows), NN).astype(BF16)

    def serve_group(gi):
        def body(j, carry):
            serve[j, gi] = serve_rows(j, gi)
            serve_copy(j, gi).start()
            return carry

        lax.fori_loop(1, NX, body, 0)

    def serve_own(gi):
        back[gi, :, 0:SLOTS] = serve_rows(0, gi)

    def relation_rows(n):
        def body(i, carry):
            lanes = pl.ds(pl.multiple_of(i * 256, 256), 256)
            pick = onehot(kind_ref[:, lanes], 0, K)
            relrow[:, lanes] = (
                dot(splits[0], pick, NN) + dot(splits[1], pick, NN) + dot(splits[2], pick, NN)
            )
            return carry

        lax.fori_loop(n, n + 1, body, 0)

    def wait_back(gi):
        for k in range(1, NX):
            remote(
                serve.at[k, gi], back.at[gi, :, lanes_of(k)], sv_s.at[k, gi], sv_r.at[k, gi], dev_x(k)
            ).wait_recv()

    def collect(gi, first):
        def body(b, carry):
            lanes = pl.ds(pl.multiple_of(b * 256, 256), 256)
            pick = onehot(place_ref[gi : gi + 1, lanes], 0, NX * SLOTS)
            rows = dot(back[gi], pick, NN).astype(BF16)
            dst[:, lanes] = rows if first else dst[:, lanes] + rows
            return carry

        lax.fori_loop(0, E // 256, body, 0)

    forward(0)
    serve_group(0)
    neg_second(0)
    serve_own(0)
    load_diag.wait()
    diag = diag_ref[...]
    high_part = diag.astype(BF16)
    rest = diag - high_part.astype(F32)
    splits[0] = high_part
    splits[1] = rest.astype(BF16)
    splits[2] = (rest - splits[1].astype(F32)).astype(BF16)
    forward(1)
    serve_group(1)
    neg_third(0)
    serve_own(1)
    relation_rows(0)
    forward(2)
    neg_fourth(0)
    relation_rows(1)
    forward(3)
    serve_group(2)
    serve_own(2)
    relation_rows(2)
    relation_rows(3)
    query[...] = (srcrow[...].astype(F32) * relrow[...]).astype(BF16)
    neg_last(0)

    scale = 1.0 / (BLOCK - 1 + NEG)
    for b in range(2):
        lanes = slice(b * BLOCK, (b + 1) * BLOCK)
        nl = slice(b * NL, (b + 1) * NL)
        q, n = query[:, lanes], neg_out[0, 0:D, nl]
        d_sampled = (scale * jax.nn.sigmoid(dot(q, n, TN))).astype(BF16)
        early[:, lanes] = dot(n, d_sampled, NT)
        neg_src[1, 0:D, nl] = dot(q, d_sampled, NN).astype(BF16)
    neg_start(1)
    for b in range(2):
        lanes = slice(b * BLOCK, (b + 1) * BLOCK)
        query_t[lanes, :] = query[:, lanes].astype(F32).T.astype(BF16)
    wait_back(0)
    collect(0, True)
    wait_back(1)
    collect(1, False)
    for half in range(2):
        at = half * H_CORE
        relbuf[at + 2000 : at + H_PART] = jnp.zeros((H_PART - 2000, 128), BF16)
        for i in range(4):
            gap = at + H_PART + i * H_Y + D
            relbuf[gap : gap + H_Y - D] = jnp.zeros((H_Y - D, 128), BF16)
    red_y[1, D:H_Y] = jnp.zeros((H_Y - D, 128), BF16)
    wait_back(2)
    collect(2, False)
    neg_second(1)

    diagonal = lax.broadcasted_iota(jnp.int32, (BLOCK, BLOCK), 0) == lax.broadcasted_iota(
        jnp.int32, (BLOCK, BLOCK), 1
    )
    for b in range(2):
        lanes = slice(b * BLOCK, (b + 1) * BLOCK)
        q, t = query[:, lanes], dst[:, lanes]
        batch = dot(query_t[lanes, :], t, NN)
        d_batch = (
            jax.nn.sigmoid(jnp.where(diagonal, -batch, batch)) * jnp.where(diagonal, -1.0, scale)
        ).astype(BF16)
        d_query = dot(t, d_batch, NT) + early[:, lanes]
        dsource[:, lanes] = (d_query * relrow[:, lanes]).astype(BF16)
        srcrow[:, lanes] = (d_query * srcrow[:, lanes].astype(F32)).astype(BF16)
        dtarget[:, lanes] = dot(q, d_batch, NN).astype(BF16)

    def relation_pair(i):
        pick = onehot(kind_ref[...], i * 256, 256)
        pair = dot(srcrow[...], pick, NT).astype(BF16)
        for half in range(2):
            at = tile_rows(half, i)
            relbuf[at : at + D] = pair[:, half * 128 : half * 128 + 128]

    def rel_rows(cc, p, yy, xx, zz, n):
        at = cc * H_CORE + p * H_PART + yy * H_Y + xx * H_X + zz * H_Z
        return pl.ds(pl.multiple_of(at, 16), n)

    def core_copy(p):
        return remote(relbuf.at[rel_rows(1 - c, p, 0, 0, 0, H_PART)], core_recv.at[p], co_s.at[0, p], co_r.at[0, p], dev_c)

    def ry_copy(p, k):
        n = Y_ROWS[p]
        return remote(
            relbuf.at[rel_rows(c, p, lax.rem(y + k, NY), 0, 0, n)], y_recv.at[p, NY - k, pl.ds(0, n)],
            ry_s.at[0, p, k], ry_r.at[0, p, NY - k], dev_y(k),
        )

    def rx_copy(p, k):
        rows = pl.ds(pl.multiple_of(lax.rem(x + k, NX) * H_X, H_X), H_X)
        return remote(red_y.at[p, rows], x_recv.at[p, NX - k], rx_s.at[0, p, k], rx_r.at[0, p, NX - k], dev_x(k))

    def rz_copy(p, k):
        rows = pl.ds(pl.multiple_of(lax.rem(z + k, NZ) * H_Z, H_Z), H_Z)
        return remote(red_x.at[p, rows], z_recv.at[p, NZ - k], rz_s.at[0, p, k], rz_r.at[0, p, NZ - k], dev_z(k))

    def rzb_copy(p, k, way):
        rows = rel_rows(c, p, y, x, lax.rem(z + k, NZ) if way else z, H_Z)
        i = k if way else NZ - k
        return remote(rel_out.at[rows], rel_out.at[rows], rz_s.at[1, p, k], rz_r.at[1, p, i], dev_z(k))

    def rxb_copy(p, k, way):
        rows = rel_rows(c, p, y, lax.rem(x + k, NX) if way else x, 0, H_X)
        i = k if way else NX - k
        return remote(rel_out.at[rows], rel_out.at[rows], rx_s.at[1, p, k], rx_r.at[1, p, i], dev_x(k))

    def ryb_copy(p, k, way):
        rows = rel_rows(c, p, lax.rem(y + k, NY) if way else y, 0, 0, Y_ROWS[p])
        i = k if way else NY - k
        return remote(rel_out.at[rows], rel_out.at[rows], ry_s.at[1, p, k], ry_r.at[1, p, i], dev_y(k))

    def cb_copy(p, way):
        rows = rel_rows(1 - c if way else c, p, 0, 0, 0, H_PART)
        return remote(rel_out.at[rows], rel_out.at[rows], co_s.at[1, p], co_r.at[1, p], dev_c)

    def rel_y(p):
        remote(core_recv.at[p], core_recv.at[p], co_s.at[0, p], co_r.at[0, p], dev_c).wait_recv()
        own = rel_rows(c, p, 0, 0, 0, H_PART)
        relbuf[own] = (relbuf[own].astype(F32) + core_recv[p].astype(F32)).astype(BF16)
        for k in range(1, NY):
            ry_copy(p, k).start()

    def rel_x(p):
        n = Y_ROWS[p]
        for k in range(1, NY):
            part = y_recv.at[p, k, pl.ds(0, n)]
            remote(part, part, ry_s.at[0, p, k], ry_r.at[0, p, k], dev_y(k)).wait_recv()
        total = relbuf[rel_rows(c, p, y, 0, 0, n)].astype(F32)
        for k in range(1, NY):
            total = total + y_recv[p, k, 0:n].astype(F32)
        red_y[p, 0:n] = total.astype(BF16)
        for k in range(1, NX):
            rx_copy(p, k).start()

    def rel_z(p):
        for k in range(1, NX):
            remote(x_recv.at[p, k], x_recv.at[p, k], rx_s.at[0, p, k], rx_r.at[0, p, k], dev_x(k)).wait_recv()
        total = red_y[p, pl.ds(pl.multiple_of(x * H_X, H_X), H_X)].astype(F32)
        for k in range(1, NX):
            total = total + x_recv[p, k].astype(F32)
        red_x[p] = total.astype(BF16)
        for k in range(1, NZ):
            rz_copy(p, k).start()

    def rel_zb(p):
        for k in range(1, NZ):
            remote(z_recv.at[p, k], z_recv.at[p, k], rz_s.at[0, p, k], rz_r.at[0, p, k], dev_z(k)).wait_recv()
        total = red_x[p, pl.ds(pl.multiple_of(z * H_Z, H_Z), H_Z)].astype(F32)
        for k in range(1, NZ):
            total = total + z_recv[p, k].astype(F32)
        rel_out[rel_rows(c, p, y, x, z, H_Z)] = total.astype(BF16)
        for k in range(1, NZ):
            rzb_copy(p, k, 0).start()

    def rel_xb(p):
        for k in range(1, NZ):
            rzb_copy(p, k, 1).wait_recv()
        for k in range(1, NX):
            rxb_copy(p, k, 0).start()

    def rel_yb(p):
        for k in range(1, NX):
            rxb_copy(p, k, 1).wait_recv()
        for k in range(1, NY):
            ryb_copy(p, k, 0).start()

    def rel_cb(p):
        for k in range(1, NY):
            ryb_copy(p, k, 1).wait_recv()
        cb_copy(p, 0).start()

    def c_copy(j, gi):
        return remote(
            serve.at[j, gi], crecv.at[gi, :, lanes_of(NX - j)], cs_s.at[j, gi], cs_r.at[NX - j, gi], dev_x(j)
        )

    def spread(j, gi):
        pick = onehot(place_ref[gi : gi + 1, :], j * SLOTS, SLOTS)
        return dot(dtarget[...], pick, NT).astype(BF16)

    def send_group(gi):
        def body(j, carry):
            serve_copy(j, gi).wait_send()
            serve[j, gi] = spread(j, gi)
            c_copy(j, gi).start()
            return carry

        lax.fori_loop(1, NX, body, 0)

    def keep_group(gi):
        crecv[gi, :, 0:SLOTS] = spread(0, gi)

    def wait_c(gi):
        for k in range(1, NX):
            remote(
                serve.at[k, gi], crecv.at[gi, :, lanes_of(k)], cs_s.at[k, gi], cs_r.at[k, gi], dev_x(k)
            ).wait_recv()

    def line_sum(offset):
        gi = [offset in members for members in GROUPS].index(True)
        li = GROUPS[gi].index(offset)
        return dot(crecv[gi], onehot(asked[gi : gi + 1, :], li * R, R), NT)

    def ring_copy(way, s, q):
        send, recv = (up_send, up_recv) if way == 0 else (down_send, down_recv)
        rows = pl.ds(*CUTS[q])
        return remote(
            send.at[s, rows], recv.at[s, rows], rs_s.at[way, s, q], rs_r.at[way, s, q],
            dev_z(1 if way == 0 else NZ - 1),
        )

    def ring_cuts(way, s):
        return range(4) if s > 0 else ((0, 1) if way == 0 else (2, 3))

    def ring_cut(s, i):
        for way in (0, 1):
            q = ((2, 3, 0, 1) if way == 0 else (0, 1, 2, 3))[i]
            if q not in ring_cuts(way, s):
                continue
            send, recv = (up_send, up_recv) if way == 0 else (down_send, down_recv)
            at, size = CUTS[q]
            rows = slice(at, at + size)
            part = lsum[0 if s == 0 else 2 * (s % 2) + way, rows]
            if s > 0 and q in ring_cuts(way, s - 1):
                ring_copy(way, s - 1, q).wait_recv()
                part = part + recv[s - 1, rows].astype(F32)
            send[s, rows] = part.astype(BF16)
            ring_copy(way, s, q).start()

    send_group(2)
    for i in range(5):
        relation_pair(i)
    core_copy(0).start()
    for i in range(5, 9):
        relation_pair(i)
    core_copy(1).start()
    rel_y(0)
    keep_group(2)
    rel_y(1)
    neg_third(1)
    first_grad[...] = dot(dsource[...], onehot(srow_ref[...], 0, R), NT)
    rel_x(0)
    wait_c(2)
    lsum[0] = line_sum(4)
    ring_cut(0, 2)
    ring_cut(0, 3)
    ring_cut(0, 0)
    ring_cut(0, 1)
    lsum[2] = line_sum(3)
    lsum[3] = line_sum(5)
    rel_z(0)
    rel_x(1)
    send_group(1)
    ring_cut(1, 0)
    ring_cut(1, 1)
    keep_group(1)
    rel_zb(0)
    rel_z(1)
    ring_cut(1, 2)
    ring_cut(1, 3)
    rel_xb(0)
    send_group(0)
    rel_zb(1)
    wait_c(1)
    lsum[0] = line_sum(2)
    lsum[1] = line_sum(6)
    ring_cut(2, 0)
    ring_cut(2, 1)
    rel_yb(0)
    rel_xb(1)
    ring_cut(2, 2)
    keep_group(0)
    ring_cut(2, 3)
    wait_c(0)
    lsum[2] = line_sum(1)
    lsum[3] = line_sum(7)
    ring_cut(3, 0)
    rel_yb(1)
    ring_cut(3, 1)
    neg_fourth(1)
    rel_cb(0)
    ring_cut(3, 2)
    ring_cut(3, 3)
    neg_last(1)
    lsum[0] = line_sum(0) + dot(neg_out[1, 0:D], onehot(negs, 0, R), NT)
    for q in range(4):
        for way in (0, 1):
            ring_copy(way, 3, q).wait_recv()
    second_grad[...] = lsum[0] + up_recv[3].astype(F32) + down_recv[3].astype(F32)
    rel_cb(1)
    cb_copy(0, 1).wait_recv()
    cb_copy(1, 1).wait_recv()

    for way in (0, 1):
        for s in range(4):
            for q in gather_cuts(way, s):
                gather_copy(way, s, q).wait_send()
            for q in ring_cuts(way, s):
                ring_copy(way, s, q).wait_send()
    for k in range(1, NX):
        req_copy(k).wait_send()
        for gi in range(3):
            c_copy(k, gi).wait_send()
    for u in range(2):
        for k in range(1, NX):
            neg_x_copy(u, k).wait_send()
            neg_xb_copy(u, k, 0).wait_send()
        for k in range(1, NZ):
            neg_z_copy(u, k).wait_send()
            neg_zb_copy(u, k, 0).wait_send()
    for p in range(2):
        core_copy(p).wait_send()
        cb_copy(p, 0).wait_send()
        for k in range(1, NY):
            ry_copy(p, k).wait_send()
            ryb_copy(p, k, 0).wait_send()
        for k in range(1, NX):
            rx_copy(p, k).wait_send()
            rxb_copy(p, k, 0).wait_send()
        for k in range(1, NZ):
            rz_copy(p, k).wait_send()
            rzb_copy(p, k, 0).wait_send()


def step_call(*args):
    vmem = pl.BlockSpec(memory_space=pltpu.VMEM)
    dma = pltpu.SemaphoreType.DMA
    return pl.pallas_call(
        step_kernel,
        out_shape=(
            jax.ShapeDtypeStruct((D, R), F32),
            jax.ShapeDtypeStruct((D, R), F32),
            jax.ShapeDtypeStruct((2 * H_CORE, 128), BF16),
        ),
        in_specs=[pl.BlockSpec(memory_space=pl.ANY) if i in (0, 2) else vmem for i in range(len(args))],
        out_specs=(vmem,) * 3,
        scratch_shapes=[
            pltpu.VMEM((D, R), F32),
            pltpu.VMEM((D, K), F32),
            pltpu.VMEM((D, NZ * R), BF16),
            pltpu.VMEM((NX, 8, SLOTS), jnp.int32),
            pltpu.VMEM((8, NX * SLOTS), jnp.int32),
            pltpu.VMEM((NX, 3, D, SLOTS), BF16),
            pltpu.VMEM((3, D, NX * SLOTS), BF16),
            pltpu.VMEM((8, E), jnp.int32),
            pltpu.VMEM((1, 2 * NL), jnp.int32),
            pltpu.VMEM((3, D, K), BF16),
            pltpu.VMEM((D, E), F32),
            pltpu.VMEM((D, E), BF16),
            pltpu.VMEM((D, E), BF16),
            pltpu.VMEM((E, D), BF16),
            pltpu.VMEM((D, E), BF16),
            pltpu.VMEM((D, E), BF16),
            pltpu.VMEM((D, E), BF16),
            pltpu.VMEM((D, E), F32),
            pltpu.VMEM((3, D, NX * SLOTS), BF16),
            pltpu.VMEM((4, D, R), BF16),
            pltpu.VMEM((4, D, R), BF16),
            pltpu.VMEM((4, D, R), BF16),
            pltpu.VMEM((4, D, R), BF16),
            pltpu.VMEM((4, D, R), F32),
            pltpu.VMEM((2, NEG_ROWS, 2 * NL), BF16),
            pltpu.VMEM((2, NX, NEG_X, 2 * NL), BF16),
            pltpu.VMEM((2, NEG_X, 2 * NL), BF16),
            pltpu.VMEM((2, NZ, NEG_Z, 2 * NL), BF16),
            pltpu.VMEM((2, NEG_ROWS, 2 * NL), BF16),
            pltpu.VMEM((2 * H_CORE, 128), BF16),
            pltpu.VMEM((2, H_PART, 128), BF16),
            pltpu.VMEM((2, NY, H_Y, 128), BF16),
            pltpu.VMEM((2, NX, H_X, 128), BF16),
            pltpu.VMEM((2, NZ, H_Z, 128), BF16),
            pltpu.VMEM((2, H_Y, 128), BF16),
            pltpu.VMEM((2, H_X, 128), BF16),
            dma((2,)),
            dma((2, 4, 4)), dma((2, 4, 4)),
            dma((NX,)), dma((NX,)),
            dma((NX, 3)), dma((NX, 3)),
            dma((NX, 3)), dma((NX, 3)),
            dma((2, 4, 4)), dma((2, 4, 4)),
            dma((2, 2, NX)), dma((2, 2, NX)),
            dma((2, 2, NZ)), dma((2, 2, NZ)),
            dma((2, 2)), dma((2, 2)),
            dma((2, 2, NY)), dma((2, 2, NY)),
            dma((2, 2, NX)), dma((2, 2, NX)),
            dma((2, 2, NZ)), dma((2, 2, NZ)),
        ],
        compiler_params=pltpu.CompilerParams(
            collective_id=0, has_side_effects=True, vmem_limit_bytes=56 * 1024 * 1024
        ),
        name="edge_step",
    )(*args)


PARTS = 3


def update_kernel(
    rel_hbm, diag, rstate_ref, first, fstate_ref, fgrad_hbm, second, sstate_ref, sgrad_hbm,
    diag_out, rstate_new, first_out, fstate_new, second_out, sstate_new,
    rel_grad, fgrad, sgrad, diag_new, first_new, second_new, in_sem, out_sem,
):
    def part(i):
        return pl.ds(i * (K // PARTS), K // PARTS)

    loads = [
        pltpu.make_async_copy(src, dst, in_sem.at[i])
        for i, (src, dst) in enumerate([(fgrad_hbm, fgrad), (sgrad_hbm, sgrad), (rel_hbm, rel_grad)])
    ]
    for load in loads:
        load.start()
    stores = [
        pltpu.make_async_copy(src, dst, out_sem.at[i])
        for i, (src, dst) in enumerate(
            [(first_new, first_out), (second_new, second_out)]
            + [(diag_new.at[:, part(i)], diag_out.at[:, part(i)]) for i in range(PARTS)]
        )
    ]
    loads[0].wait()
    first_new[...], fstate_new[...] = adagrad(first[...], fstate_ref[...], fgrad[...])
    stores[0].start()
    loads[1].wait()
    second_new[...], sstate_new[...] = adagrad(second[...], sstate_ref[...], sgrad[...])
    stores[1].start()
    loads[2].wait()
    for i in range(9):
        for half in range(2):
            at = tile_rows(half, i)
            lanes = slice((2 * i + half) * 128, (2 * i + half + 1) * 128)
            grad = rel_grad[at : at + D].astype(F32)
            diag_new[:, lanes], state = adagrad(diag[:, lanes], rstate_ref[lanes].reshape(1, 128), grad)
            rstate_new[lanes] = state.reshape(128)
        if i % (9 // PARTS) == 9 // PARTS - 1:
            stores[2 + i // (9 // PARTS)].start()
    for store in stores:
        store.wait()


def update_call(rel_grad, diag, rstate, first, fstate, first_grad, second, sstate, second_grad):
    shape = jax.ShapeDtypeStruct
    vmem, hbm = pl.BlockSpec(memory_space=pltpu.VMEM), pl.BlockSpec(memory_space=pltpu.HBM)
    table = pltpu.VMEM((D, R), F32)
    return pl.pallas_call(
        update_kernel,
        out_shape=(
            shape((D, K), F32), shape((K,), F32), shape((D, R), F32), shape((1, R), F32),
            shape((D, R), F32), shape((1, R), F32),
        ),
        in_specs=[hbm, vmem, vmem, vmem, vmem, hbm, vmem, vmem, hbm],
        out_specs=(hbm, vmem, hbm, vmem, hbm, vmem),
        scratch_shapes=[
            pltpu.VMEM((2 * H_CORE, 128), BF16), table, table, pltpu.VMEM((D, K), F32), table, table,
            pltpu.SemaphoreType.DMA((3,)), pltpu.SemaphoreType.DMA((2 + PARTS,)),
        ],
        compiler_params=pltpu.CompilerParams(vmem_limit_bytes=24 * 1024 * 1024),
        name="table_update",
    )(rel_grad, diag, rstate, first, fstate, first_grad, second, sstate, second_grad)


def on_device(
    first_table, first_state, second_table, second_state, relation_diag, relation_state,
    source_row, target_owner, target_row, relation_id, negative_id,
):
    diag, first, second = relation_diag.T, first_table[0].T, second_table[0].T
    first_grad, second_grad, rel_grad = step_call(
        first, second, diag,
        source_row, target_owner.reshape(1, E), target_row, relation_id, negative_id[0],
    )
    first_grad, second_grad, rel_grad = (
        pltpu.with_memory_space_constraint(v, pltpu.HBM) for v in (first_grad, second_grad, rel_grad)
    )
    diag_new, state_new, first_new, first_state_new, second_new, second_state_new = update_call(
        rel_grad, diag, relation_state, first, first_state, first_grad, second, second_state, second_grad
    )
    return (
        first_new.T[None], first_state_new, second_new.T[None], second_state_new,
        diag_new.T, state_new,
    )


def solution(mesh):
    in_specs = (
        P("group", "owner", None),
        P("group", "owner"),
        P("group", "owner", None),
        P("group", "owner"),
        P(),
        P(),
        P("group", "owner"),
        P("group", "owner", None),
        P("group", "owner"),
        P("group", "owner"),
        P("group", None, None),
    )
    out_specs = (
        P("group", "owner", None),
        P("group", "owner"),
        P("group", "owner", None),
        P("group", "owner"),
        P(),
        P(),
    )
    return jax.shard_map(
        on_device, mesh=mesh, in_specs=in_specs, out_specs=out_specs, check_vma=False
    )
```

```python
import jax
import jax.numpy as jnp
from jax import lax
from jax.experimental import pallas as pl
from jax.experimental.pallas import tpu as pltpu
from jax.sharding import PartitionSpec as P

MESH = pl.DeviceIdType.MESH
F32 = jnp.float32
BF16 = jnp.bfloat16
LEARN = 0.1

D = 400
R = 512
E = 1024
BLOCK = 512
NEG = 100
NL = 128
K = 2304
NX, NY, NZ = 4, 4, 8
SLOTS = 256

GROUPS = ((7, 0, 1), (2, 6), (3, 4, 5))
SPOT = (1, 2, 3, 5, 6, 7, 4, 0)
CUTS = ((0, 96), (96, 112), (208, 96), (304, 96))
UP = (0, 7, 6, 5, 4)
DOWN = (0, 1, 2, 3, 4)
HALF = 208

H_CORE, H_PART, H_Y, H_X, H_Z = 4096, 2048, 512, 128, 16
Y_ROWS = (512, 400)
NEG_X, NEG_Z = 128, 16
NEG_ROWS = 512


def tile_rows(half, i):
    return half * H_CORE + (i * D if i < 5 else H_PART + (i - 5) * H_Y)


NN = (((1,), (0,)), ((), ()))
NT = (((1,), (1,)), ((), ()))
TN = (((0,), (0,)), ((), ()))


def dot(a, b, dims):
    return lax.dot_general(a, b, dims, preferred_element_type=F32)


def onehot(vec, base, n):
    rows = lax.broadcasted_iota(jnp.int32, (n, vec.shape[1]), 0)
    return jnp.where(rows == vec - base, 1.0, 0.0).astype(BF16)


def adagrad(table, state, grad):
    state_new = state + jnp.sum(grad * grad, axis=0, keepdims=True) * (1.0 / D)
    return table - LEARN * grad * (1.0 / jnp.sqrt(state_new)), state_new


def step_kernel(
    first_hbm, second_ref, diag_hbm, srow_ref, towner_ref, trow_ref, kind_ref, neg_ref,
    first_hbm_out, second_hbm_out, rel_hbm_out,
    first_ref, diag_ref, first_grad, second_grad, rel_out, tabs, req, asked, serve, back, place_ref, neg_ids,
    splits, relrow, srcrow, query, query_t, dst, dsource, dtarget, early,
    crecv, up_send, up_recv, down_send, down_recv, lsum,
    neg_src, neg_xr, neg_xs, neg_zr, neg_out,
    relbuf, core_recv, y_recv, x_recv, z_recv, red_y, red_x,
    dg_s, ag_s, ag_r, rq_s, rq_r, sv_s, sv_r, cs_s, cs_r, rs_s, rs_r, nx_s, nx_r, nz_s, nz_r,
    co_s, co_r, ry_s, ry_r, rx_s, rx_r, rz_s, rz_r,
):
    g = lax.axis_index("group")
    o = lax.axis_index("owner")
    x, z = o // NZ, o % NZ
    y, c = g // 2, g % 2

    def dev_x(k):
        return (g, lax.rem(x + k, NX) * NZ + z)

    def dev_z(k):
        return (g, x * NZ + lax.rem(z + k, NZ))

    def dev_y(k):
        return (lax.rem(y + k, NY) * 2 + c, o)

    dev_c = (y * 2 + 1 - c, o)

    barrier = pltpu.get_barrier_semaphore()
    for peer in [dev_x(k) for k in range(1, NX)] + [dev_z(k) for k in range(1, NZ)] + [
        dev_y(k) for k in range(1, NY)
    ] + [dev_c]:
        pl.semaphore_signal(barrier, inc=1, device_id=peer, device_id_type=MESH)
    load_diag = pltpu.make_async_copy(diag_hbm, diag_ref, dg_s.at[0])
    load_first = pltpu.make_async_copy(first_hbm, first_ref, dg_s.at[1])
    load_first.start()
    load_diag.start()
    def table_lanes(offset):
        return pl.ds(SPOT[offset] * R, R)

    tabs[:, table_lanes(0)] = second_ref[...].astype(BF16)
    pl.semaphore_wait(barrier, NX + NZ + NY - 3 + 1)

    def remote(src, dst_, ss, rs, dev):
        return pltpu.make_async_remote_copy(
            src_ref=src, dst_ref=dst_, send_sem=ss, recv_sem=rs, device_id=dev, device_id_type=MESH
        )

    def gather_copy(way, step, q):
        path = UP if way == 0 else DOWN
        rows = pl.ds(*CUTS[q])
        return remote(
            tabs.at[rows, table_lanes(path[step])], tabs.at[rows, table_lanes(path[step + 1])],
            ag_s.at[way, step, q], ag_r.at[way, step, q], dev_z(1 if way == 0 else NZ - 1),
        )

    def gather_cuts(way, step):
        return range(4) if step < 3 else ((0, 1) if way == 0 else (2, 3))

    for q in range(4):
        for way in (0, 1):
            gather_copy(way, 0, q).start()

    def forward(step):
        for q in range(4):
            for way in (0, 1):
                if q in gather_cuts(way, step):
                    gather_copy(way, step, q).wait_recv()
                    if step < 3 and q in gather_cuts(way, step + 1):
                        gather_copy(way, step + 1, q).start()

    towner, trow = towner_ref[...], trow_ref[...]
    far = lax.rem(towner % NZ - z + NZ, NZ)
    side = lax.rem(towner // NZ - x + NX, NX)
    group = jnp.zeros_like(far)
    local = jnp.zeros_like(far)
    for gi, members in enumerate(GROUPS):
        for li, offset in enumerate(members):
            group = jnp.where(far == offset, gi, group)
            local = jnp.where(far == offset, li, local)
    kind_of = side * 8 + group
    mine = jnp.where(lax.broadcasted_iota(jnp.int32, (32, E), 0) == kind_of, 1.0, 0.0)
    before_mask = jnp.where(
        lax.broadcasted_iota(jnp.int32, (E, E), 0) < lax.broadcasted_iota(jnp.int32, (E, E), 1), 1.0, 0.0
    ).astype(BF16)
    before = dot(mine.astype(BF16), before_mask, NN)
    slot = jnp.sum(mine * before, axis=0, keepdims=True).astype(jnp.int32)
    for gi in range(3):
        place_ref[gi : gi + 1, :] = jnp.where(group == gi, side * SLOTS + slot, -1)
    value = local * R + trow + 1
    high = (value // 16).astype(F32)
    low = (value % 16).astype(F32)
    sends = jnp.concatenate([mine * high, mine * low], axis=0).astype(BF16)
    found = dot(sends, onehot(slot, 0, SLOTS), NT)
    wanted = (found[0:32] * 16.0 + found[32:64]).astype(jnp.int32) - 1
    asked[:, 0:SLOTS] = wanted[0:8]
    for k in range(1, NX):
        req[k] = wanted[8 * k : 8 * k + 8]

    def req_copy(k):
        return remote(req.at[k], asked.at[:, pl.ds((NX - k) * SLOTS, SLOTS)], rq_s.at[k], rq_r.at[NX - k], dev_x(k))

    for k in range(1, NX):
        req_copy(k).start()

    def neg_x_copy(u, k):
        rows = pl.ds(pl.multiple_of(lax.rem(x + k, NX) * NEG_X, NEG_X), NEG_X)
        return remote(neg_src.at[u, rows], neg_xr.at[u, NX - k], nx_s.at[u, 0, k], nx_r.at[u, 0, NX - k], dev_x(k))

    def neg_z_copy(u, k):
        rows = pl.ds(pl.multiple_of(lax.rem(z + k, NZ) * NEG_Z, NEG_Z), NEG_Z)
        return remote(neg_xs.at[u, rows], neg_zr.at[u, NZ - k], nz_s.at[u, 0, k], nz_r.at[u, 0, NZ - k], dev_z(k))

    def neg_zb_copy(u, k, way):
        at = lax.rem(z + k, NZ) if way else z
        rows = pl.ds(pl.multiple_of(x * NEG_X + at * NEG_Z, NEG_Z), NEG_Z)
        i = k if way else NZ - k
        return remote(neg_out.at[u, rows], neg_out.at[u, rows], nz_s.at[u, 1, k], nz_r.at[u, 1, i], dev_z(k))

    def neg_xb_copy(u, k, way):
        at = lax.rem(x + k, NX) if way else x
        rows = pl.ds(pl.multiple_of(at * NEG_X, NEG_X), NEG_X)
        i = k if way else NX - k
        return remote(neg_out.at[u, rows], neg_out.at[u, rows], nx_s.at[u, 1, k], nx_r.at[u, 1, i], dev_x(k))

    def neg_start(u):
        for k in range(1, NX):
            neg_x_copy(u, k).start()

    def neg_second(u):
        for k in range(1, NX):
            remote(neg_xr.at[u, k], neg_xr.at[u, k], nx_s.at[u, 0, k], nx_r.at[u, 0, k], dev_x(k)).wait_recv()
        total = neg_src[u, pl.ds(pl.multiple_of(x * NEG_X, NEG_X), NEG_X)].astype(F32)
        for k in range(1, NX):
            total = total + neg_xr[u, k].astype(F32)
        neg_xs[u] = total.astype(BF16)
        for k in range(1, NZ):
            neg_z_copy(u, k).start()

    def neg_third(u):
        for k in range(1, NZ):
            remote(neg_zr.at[u, k], neg_zr.at[u, k], nz_s.at[u, 0, k], nz_r.at[u, 0, k], dev_z(k)).wait_recv()
        total = neg_xs[u, pl.ds(pl.multiple_of(z * NEG_Z, NEG_Z), NEG_Z)].astype(F32)
        for k in range(1, NZ):
            total = total + neg_zr[u, k].astype(F32)
        neg_out[u, pl.ds(pl.multiple_of(x * NEG_X + z * NEG_Z, NEG_Z), NEG_Z)] = total.astype(BF16)
        for k in range(1, NZ):
            neg_zb_copy(u, k, 0).start()

    def neg_fourth(u):
        for k in range(1, NZ):
            neg_zb_copy(u, k, 1).wait_recv()
        for k in range(1, NX):
            neg_xb_copy(u, k, 0).start()

    def neg_last(u):
        for k in range(1, NX):
            neg_xb_copy(u, k, 1).wait_recv()

    neg_ids[...] = jnp.full((1, 2 * NL), -(1 << 20), jnp.int32)
    for b in range(2):
        neg_ids[:, b * NL : b * NL + NEG] = neg_ref[b : b + 1, :]
    negs = neg_ids[...] - o * R
    neg_src[0, 0:D] = dot(tabs[:, table_lanes(0)], onehot(negs, 0, R), NN).astype(BF16)
    for u in range(2):
        neg_src[u, D:NEG_ROWS] = jnp.zeros((NEG_ROWS - D, 2 * NL), BF16)
    neg_start(0)

    load_first.wait()
    first_copy = first_ref[...].astype(BF16)
    for b in range(2):
        lanes = slice(b * BLOCK, (b + 1) * BLOCK)
        srcrow[:, lanes] = dot(first_copy, onehot(srow_ref[:, lanes], 0, R), NN).astype(BF16)

    for k in range(1, NX):
        remote(req.at[k], asked.at[:, pl.ds(k * SLOTS, SLOTS)], rq_s.at[k], rq_r.at[k], dev_x(k)).wait_recv()

    def lanes_of(j):
        start = j * SLOTS
        return pl.ds(start if isinstance(j, int) else pl.multiple_of(start, SLOTS), SLOTS)

    def serve_copy(j, gi):
        return remote(
            serve.at[j, gi], back.at[gi, :, lanes_of(NX - j)], sv_s.at[j, gi], sv_r.at[NX - j, gi], dev_x(j)
        )

    def serve_rows(j, gi):
        members = GROUPS[gi]
        start = SPOT[members[0]] * R
        rows = len(members) * R
        want = asked[gi : gi + 1, lanes_of(j)]
        return dot(tabs[:, start : start + rows], onehot(want, 0, rows), NN).astype(BF16)

    def serve_group(gi):
        def body(i, carry):
            j = 2 - i + 3 * (i // 2)
            serve[j, gi] = serve_rows(j, gi)
            serve_copy(j, gi).start()
            return carry

        lax.fori_loop(0, NX - 1, body, 0)

    def serve_own(gi):
        back[gi, :, 0:SLOTS] = serve_rows(0, gi)

    def relation_rows(n):
        def body(i, carry):
            lanes = pl.ds(pl.multiple_of(i * 256, 256), 256)
            pick = onehot(kind_ref[:, lanes], 0, K)
            relrow[:, lanes] = (
                dot(splits[0], pick, NN) + dot(splits[1], pick, NN) + dot(splits[2], pick, NN)
            )
            return carry

        lax.fori_loop(n, n + 1, body, 0)

    def wait_back(gi):
        for k in range(1, NX):
            remote(
                serve.at[k, gi], back.at[gi, :, lanes_of(k)], sv_s.at[k, gi], sv_r.at[k, gi], dev_x(k)
            ).wait_recv()

    def collect(gi, first):
        def body(b, carry):
            lanes = pl.ds(pl.multiple_of(b * 256, 256), 256)
            pick = onehot(place_ref[gi : gi + 1, lanes], 0, NX * SLOTS)
            rows = dot(back[gi], pick, NN).astype(BF16)
            dst[:, lanes] = rows if first else dst[:, lanes] + rows
            return carry

        lax.fori_loop(0, E // 256, body, 0)

    forward(0)
    serve_group(0)
    neg_second(0)
    serve_own(0)
    load_diag.wait()
    diag = diag_ref[...]
    high_part = diag.astype(BF16)
    rest = diag - high_part.astype(F32)
    splits[0] = high_part
    splits[1] = rest.astype(BF16)
    splits[2] = (rest - splits[1].astype(F32)).astype(BF16)
    forward(1)
    serve_group(1)
    neg_third(0)
    serve_own(1)
    relation_rows(0)
    neg_fourth(0)
    forward(2)
    relation_rows(1)
    forward(3)
    serve_group(2)
    serve_own(2)
    relation_rows(2)
    relation_rows(3)
    query[...] = (srcrow[...].astype(F32) * relrow[...]).astype(BF16)
    neg_last(0)

    scale = 1.0 / (BLOCK - 1 + NEG)
    for b in range(2):
        lanes = slice(b * BLOCK, (b + 1) * BLOCK)
        nl = slice(b * NL, (b + 1) * NL)
        q, n = query[:, lanes], neg_out[0, 0:D, nl]
        d_sampled = (scale * jax.nn.sigmoid(dot(q, n, TN))).astype(BF16)
        early[:, lanes] = dot(n, d_sampled, NT)
        neg_src[1, 0:D, nl] = dot(q, d_sampled, NN).astype(BF16)
    neg_start(1)
    for b in range(2):
        lanes = slice(b * BLOCK, (b + 1) * BLOCK)
        query_t[lanes, :] = query[:, lanes].astype(F32).T.astype(BF16)
    wait_back(0)
    collect(0, True)
    wait_back(1)
    collect(1, False)
    for half in range(2):
        at = half * H_CORE
        relbuf[at + 2000 : at + H_PART] = jnp.zeros((H_PART - 2000, 128), BF16)
        for i in range(4):
            gap = at + H_PART + i * H_Y + D
            relbuf[gap : gap + H_Y - D] = jnp.zeros((H_Y - D, 128), BF16)
    red_y[1, D:H_Y] = jnp.zeros((H_Y - D, 128), BF16)
    wait_back(2)
    collect(2, False)
    neg_second(1)

    diagonal = lax.broadcasted_iota(jnp.int32, (BLOCK, BLOCK), 0) == lax.broadcasted_iota(
        jnp.int32, (BLOCK, BLOCK), 1
    )
    for b in range(2):
        lanes = slice(b * BLOCK, (b + 1) * BLOCK)
        q, t = query[:, lanes], dst[:, lanes]
        batch = dot(query_t[lanes, :], t, NN)
        d_batch = (
            jax.nn.sigmoid(jnp.where(diagonal, -batch, batch)) * jnp.where(diagonal, -1.0, scale)
        ).astype(BF16)
        d_query = dot(t, d_batch, NT) + early[:, lanes]
        dsource[:, lanes] = (d_query * relrow[:, lanes]).astype(BF16)
        srcrow[:, lanes] = (d_query * srcrow[:, lanes].astype(F32)).astype(BF16)
        dtarget[:, lanes] = dot(q, d_batch, NN).astype(BF16)

    def relation_pair(i):
        pick = onehot(kind_ref[...], i * 256, 256)
        pair = dot(srcrow[...], pick, NT).astype(BF16)
        for half in range(2):
            at = tile_rows(half, i)
            relbuf[at : at + D] = pair[:, half * 128 : half * 128 + 128]

    def rel_rows(cc, p, yy, xx, zz, n):
        at = cc * H_CORE + p * H_PART + yy * H_Y + xx * H_X + zz * H_Z
        return pl.ds(pl.multiple_of(at, 16), n)

    def core_copy(p):
        return remote(relbuf.at[rel_rows(1 - c, p, 0, 0, 0, H_PART)], core_recv.at[p], co_s.at[0, p], co_r.at[0, p], dev_c)

    def ry_copy(p, k):
        n = Y_ROWS[p]
        return remote(
            relbuf.at[rel_rows(c, p, lax.rem(y + k, NY), 0, 0, n)], y_recv.at[p, NY - k, pl.ds(0, n)],
            ry_s.at[0, p, k], ry_r.at[0, p, NY - k], dev_y(k),
        )

    def rx_copy(p, k):
        rows = pl.ds(pl.multiple_of(lax.rem(x + k, NX) * H_X, H_X), H_X)
        return remote(red_y.at[p, rows], x_recv.at[p, NX - k], rx_s.at[0, p, k], rx_r.at[0, p, NX - k], dev_x(k))

    def rz_copy(p, k):
        rows = pl.ds(pl.multiple_of(lax.rem(z + k, NZ) * H_Z, H_Z), H_Z)
        return remote(red_x.at[p, rows], z_recv.at[p, NZ - k], rz_s.at[0, p, k], rz_r.at[0, p, NZ - k], dev_z(k))

    def rzb_copy(p, k, way):
        rows = rel_rows(c, p, y, x, lax.rem(z + k, NZ) if way else z, H_Z)
        i = k if way else NZ - k
        return remote(rel_out.at[rows], rel_out.at[rows], rz_s.at[1, p, k], rz_r.at[1, p, i], dev_z(k))

    def rxb_copy(p, k, way):
        rows = rel_rows(c, p, y, lax.rem(x + k, NX) if way else x, 0, H_X)
        i = k if way else NX - k
        return remote(rel_out.at[rows], rel_out.at[rows], rx_s.at[1, p, k], rx_r.at[1, p, i], dev_x(k))

    def ryb_copy(p, k, way):
        rows = rel_rows(c, p, lax.rem(y + k, NY) if way else y, 0, 0, Y_ROWS[p])
        i = k if way else NY - k
        return remote(rel_out.at[rows], rel_out.at[rows], ry_s.at[1, p, k], ry_r.at[1, p, i], dev_y(k))

    def cb_copy(p, way):
        rows = rel_rows(1 - c if way else c, p, 0, 0, 0, H_PART)
        return remote(rel_out.at[rows], rel_out.at[rows], co_s.at[1, p], co_r.at[1, p], dev_c)

    def rel_y(p):
        remote(core_recv.at[p], core_recv.at[p], co_s.at[0, p], co_r.at[0, p], dev_c).wait_recv()
        own = rel_rows(c, p, 0, 0, 0, H_PART)
        relbuf[own] = (relbuf[own].astype(F32) + core_recv[p].astype(F32)).astype(BF16)
        for k in range(1, NY):
            ry_copy(p, k).start()

    def rel_x(p):
        n = Y_ROWS[p]
        for k in range(1, NY):
            part = y_recv.at[p, k, pl.ds(0, n)]
            remote(part, part, ry_s.at[0, p, k], ry_r.at[0, p, k], dev_y(k)).wait_recv()
        total = relbuf[rel_rows(c, p, y, 0, 0, n)].astype(F32)
        for k in range(1, NY):
            total = total + y_recv[p, k, 0:n].astype(F32)
        red_y[p, 0:n] = total.astype(BF16)
        for k in range(1, NX):
            rx_copy(p, k).start()

    def rel_z(p):
        for k in range(1, NX):
            remote(x_recv.at[p, k], x_recv.at[p, k], rx_s.at[0, p, k], rx_r.at[0, p, k], dev_x(k)).wait_recv()
        total = red_y[p, pl.ds(pl.multiple_of(x * H_X, H_X), H_X)].astype(F32)
        for k in range(1, NX):
            total = total + x_recv[p, k].astype(F32)
        red_x[p] = total.astype(BF16)
        for k in range(1, NZ):
            rz_copy(p, k).start()

    def rel_zb(p):
        for k in range(1, NZ):
            remote(z_recv.at[p, k], z_recv.at[p, k], rz_s.at[0, p, k], rz_r.at[0, p, k], dev_z(k)).wait_recv()
        total = red_x[p, pl.ds(pl.multiple_of(z * H_Z, H_Z), H_Z)].astype(F32)
        for k in range(1, NZ):
            total = total + z_recv[p, k].astype(F32)
        rel_out[rel_rows(c, p, y, x, z, H_Z)] = total.astype(BF16)
        for k in range(1, NZ):
            rzb_copy(p, k, 0).start()

    def rel_xb(p):
        for k in range(1, NZ):
            rzb_copy(p, k, 1).wait_recv()
        for k in range(1, NX):
            rxb_copy(p, k, 0).start()

    def rel_yb(p):
        for k in range(1, NX):
            rxb_copy(p, k, 1).wait_recv()
        for k in range(1, NY):
            ryb_copy(p, k, 0).start()

    def rel_cb(p):
        for k in range(1, NY):
            ryb_copy(p, k, 1).wait_recv()
        cb_copy(p, 0).start()

    def c_copy(j, gi):
        return remote(
            serve.at[j, gi], crecv.at[gi, :, lanes_of(NX - j)], cs_s.at[j, gi], cs_r.at[NX - j, gi], dev_x(j)
        )

    def spread(j, gi):
        pick = onehot(place_ref[gi : gi + 1, :], j * SLOTS, SLOTS)
        return dot(dtarget[...], pick, NT).astype(BF16)

    def send_group(gi):
        def body(i, carry):
            j = 2 - i + 3 * (i // 2)
            serve_copy(j, gi).wait_send()
            serve[j, gi] = spread(j, gi)
            c_copy(j, gi).start()
            return carry

        lax.fori_loop(0, NX - 1, body, 0)

    def keep_group(gi):
        crecv[gi, :, 0:SLOTS] = spread(0, gi)

    def wait_c(gi):
        for k in range(1, NX):
            remote(
                serve.at[k, gi], crecv.at[gi, :, lanes_of(k)], cs_s.at[k, gi], cs_r.at[k, gi], dev_x(k)
            ).wait_recv()

    def line_sum(offset):
        gi = [offset in members for members in GROUPS].index(True)
        li = GROUPS[gi].index(offset)
        return dot(crecv[gi], onehot(asked[gi : gi + 1, :], li * R, R), NT)

    def ring_copy(way, s, q):
        send, recv = (up_send, up_recv) if way == 0 else (down_send, down_recv)
        rows = pl.ds(*CUTS[q])
        return remote(
            send.at[s, rows], recv.at[s, rows], rs_s.at[way, s, q], rs_r.at[way, s, q],
            dev_z(1 if way == 0 else NZ - 1),
        )

    def ring_cuts(way, s):
        return range(4) if s > 0 else ((0, 1) if way == 0 else (2, 3))

    def ring_cut(s, i):
        for way in (0, 1):
            q = ((2, 3, 0, 1) if way == 0 else (0, 1, 2, 3))[i]
            if q not in ring_cuts(way, s):
                continue
            send, recv = (up_send, up_recv) if way == 0 else (down_send, down_recv)
            at, size = CUTS[q]
            rows = slice(at, at + size)
            part = lsum[0 if s == 0 else 2 * (s % 2) + way, rows]
            if s > 0 and q in ring_cuts(way, s - 1):
                ring_copy(way, s - 1, q).wait_recv()
                part = part + recv[s - 1, rows].astype(F32)
            send[s, rows] = part.astype(BF16)
            ring_copy(way, s, q).start()

    for i in range(5):
        relation_pair(i)
    core_copy(0).start()
    send_group(2)
    for i in range(5, 9):
        relation_pair(i)
    core_copy(1).start()
    rel_y(0)
    keep_group(2)
    rel_y(1)
    neg_third(1)
    first_grad[...] = dot(dsource[...], onehot(srow_ref[...], 0, R), NT)
    keep_first = pltpu.make_async_copy(first_grad, first_hbm_out, dg_s.at[2])
    keep_first.start()
    rel_x(0)
    wait_c(2)
    lsum[0] = line_sum(4)
    ring_cut(0, 2)
    ring_cut(0, 3)
    ring_cut(0, 0)
    ring_cut(0, 1)
    lsum[2] = line_sum(3)
    lsum[3] = line_sum(5)
    rel_z(0)
    rel_x(1)
    send_group(1)
    ring_cut(1, 0)
    ring_cut(1, 1)
    keep_group(1)
    rel_zb(0)
    rel_z(1)
    ring_cut(1, 2)
    ring_cut(1, 3)
    rel_xb(0)
    send_group(0)
    rel_zb(1)
    wait_c(1)
    lsum[0] = line_sum(2)
    lsum[1] = line_sum(6)
    ring_cut(2, 0)
    ring_cut(2, 1)
    rel_yb(0)
    rel_xb(1)
    ring_cut(2, 2)
    keep_group(0)
    ring_cut(2, 3)
    wait_c(0)
    lsum[2] = line_sum(1)
    lsum[3] = line_sum(7)
    ring_cut(3, 0)
    rel_yb(1)
    ring_cut(3, 1)
    neg_fourth(1)
    rel_cb(0)
    ring_cut(3, 2)
    ring_cut(3, 3)
    neg_last(1)
    lsum[0] = line_sum(0) + dot(neg_out[1, 0:D], onehot(negs, 0, R), NT)
    for q in range(4):
        for way in (0, 1):
            ring_copy(way, 3, q).wait_recv()
    second_grad[...] = lsum[0] + up_recv[3].astype(F32) + down_recv[3].astype(F32)
    keep_second = pltpu.make_async_copy(second_grad, second_hbm_out, dg_s.at[3])
    keep_second.start()

    def keep_rel(p, theirs):
        rows = rel_rows(1 - c if theirs else c, p, 0, 0, 0, H_PART)
        return pltpu.make_async_copy(rel_out.at[rows], rel_hbm_out.at[rows], dg_s.at[4 + 2 * p + theirs])

    rel_cb(1)
    keep_rel(0, 0).start()
    keep_rel(1, 0).start()
    cb_copy(0, 1).wait_recv()
    keep_rel(0, 1).start()
    cb_copy(1, 1).wait_recv()
    keep_rel(1, 1).start()

    for way in (0, 1):
        for s in range(4):
            for q in gather_cuts(way, s):
                gather_copy(way, s, q).wait_send()
            for q in ring_cuts(way, s):
                ring_copy(way, s, q).wait_send()
    for k in range(1, NX):
        req_copy(k).wait_send()
        for gi in range(3):
            c_copy(k, gi).wait_send()
    for u in range(2):
        for k in range(1, NX):
            neg_x_copy(u, k).wait_send()
            neg_xb_copy(u, k, 0).wait_send()
        for k in range(1, NZ):
            neg_z_copy(u, k).wait_send()
            neg_zb_copy(u, k, 0).wait_send()
    for p in range(2):
        core_copy(p).wait_send()
        cb_copy(p, 0).wait_send()
        for k in range(1, NY):
            ry_copy(p, k).wait_send()
            ryb_copy(p, k, 0).wait_send()
        for k in range(1, NX):
            rx_copy(p, k).wait_send()
            rxb_copy(p, k, 0).wait_send()
        for k in range(1, NZ):
            rz_copy(p, k).wait_send()
            rzb_copy(p, k, 0).wait_send()
    keep_first.wait()
    keep_second.wait()
    for p in range(2):
        keep_rel(p, 0).wait()
        keep_rel(p, 1).wait()


def step_call(*args):
    vmem = pl.BlockSpec(memory_space=pltpu.VMEM)
    dma = pltpu.SemaphoreType.DMA
    return pl.pallas_call(
        step_kernel,
        out_shape=(
            jax.ShapeDtypeStruct((D, R), F32),
            jax.ShapeDtypeStruct((D, R), F32),
            jax.ShapeDtypeStruct((2 * H_CORE, 128), BF16),
        ),
        in_specs=[pl.BlockSpec(memory_space=pl.ANY) if i in (0, 2) else vmem for i in range(len(args))],
        out_specs=(pl.BlockSpec(memory_space=pl.ANY),) * 3,
        scratch_shapes=[
            pltpu.VMEM((D, R), F32),
            pltpu.VMEM((D, K), F32),
            pltpu.VMEM((D, R), F32),
            pltpu.VMEM((D, R), F32),
            pltpu.VMEM((2 * H_CORE, 128), BF16),
            pltpu.VMEM((D, NZ * R), BF16),
            pltpu.VMEM((NX, 8, SLOTS), jnp.int32),
            pltpu.VMEM((8, NX * SLOTS), jnp.int32),
            pltpu.VMEM((NX, 3, D, SLOTS), BF16),
            pltpu.VMEM((3, D, NX * SLOTS), BF16),
            pltpu.VMEM((8, E), jnp.int32),
            pltpu.VMEM((1, 2 * NL), jnp.int32),
            pltpu.VMEM((3, D, K), BF16),
            pltpu.VMEM((D, E), F32),
            pltpu.VMEM((D, E), BF16),
            pltpu.VMEM((D, E), BF16),
            pltpu.VMEM((E, D), BF16),
            pltpu.VMEM((D, E), BF16),
            pltpu.VMEM((D, E), BF16),
            pltpu.VMEM((D, E), BF16),
            pltpu.VMEM((D, E), F32),
            pltpu.VMEM((3, D, NX * SLOTS), BF16),
            pltpu.VMEM((4, D, R), BF16),
            pltpu.VMEM((4, D, R), BF16),
            pltpu.VMEM((4, D, R), BF16),
            pltpu.VMEM((4, D, R), BF16),
            pltpu.VMEM((4, D, R), F32),
            pltpu.VMEM((2, NEG_ROWS, 2 * NL), BF16),
            pltpu.VMEM((2, NX, NEG_X, 2 * NL), BF16),
            pltpu.VMEM((2, NEG_X, 2 * NL), BF16),
            pltpu.VMEM((2, NZ, NEG_Z, 2 * NL), BF16),
            pltpu.VMEM((2, NEG_ROWS, 2 * NL), BF16),
            pltpu.VMEM((2 * H_CORE, 128), BF16),
            pltpu.VMEM((2, H_PART, 128), BF16),
            pltpu.VMEM((2, NY, H_Y, 128), BF16),
            pltpu.VMEM((2, NX, H_X, 128), BF16),
            pltpu.VMEM((2, NZ, H_Z, 128), BF16),
            pltpu.VMEM((2, H_Y, 128), BF16),
            pltpu.VMEM((2, H_X, 128), BF16),
            dma((8,)),
            dma((2, 4, 4)), dma((2, 4, 4)),
            dma((NX,)), dma((NX,)),
            dma((NX, 3)), dma((NX, 3)),
            dma((NX, 3)), dma((NX, 3)),
            dma((2, 4, 4)), dma((2, 4, 4)),
            dma((2, 2, NX)), dma((2, 2, NX)),
            dma((2, 2, NZ)), dma((2, 2, NZ)),
            dma((2, 2)), dma((2, 2)),
            dma((2, 2, NY)), dma((2, 2, NY)),
            dma((2, 2, NX)), dma((2, 2, NX)),
            dma((2, 2, NZ)), dma((2, 2, NZ)),
        ],
        compiler_params=pltpu.CompilerParams(
            collective_id=0, has_side_effects=True, vmem_limit_bytes=56 * 1024 * 1024
        ),
        name="edge_step",
    )(*args)


PARTS = 9


def update_kernel(
    rel_hbm, diag, rstate_ref, first, fstate_ref, fgrad_hbm, second, sstate_ref, sgrad_hbm,
    diag_out, rstate_new, first_out, fstate_new, second_out, sstate_new,
    rel_grad, fgrad, sgrad, diag_new, first_new, second_new, in_sem, out_sem,
):
    def part(i):
        return pl.ds(i * (K // PARTS), K // PARTS)

    loads = [
        pltpu.make_async_copy(src, dst, in_sem.at[i])
        for i, (src, dst) in enumerate(
            [
                (rel_hbm.at[pl.ds(h * H_CORE + p * H_PART, H_PART)], rel_grad.at[pl.ds(h * H_CORE + p * H_PART, H_PART)])
                for p in range(2)
                for h in range(2)
            ]
            + [(fgrad_hbm, fgrad), (sgrad_hbm, sgrad)]
        )
    ]
    for load in loads:
        load.start()
    stores = [
        pltpu.make_async_copy(src, dst, out_sem.at[i])
        for i, (src, dst) in enumerate(
            [(first_new, first_out), (second_new, second_out)]
            + [(diag_new.at[:, part(i)], diag_out.at[:, part(i)]) for i in range(PARTS)]
        )
    ]
    for i in range(9):
        if i in (0, 5):
            loads[2 * (i // 5)].wait()
            loads[2 * (i // 5) + 1].wait()
        for half in range(2):
            at = tile_rows(half, i)
            lanes = slice((2 * i + half) * 128, (2 * i + half + 1) * 128)
            grad = rel_grad[at : at + D].astype(F32)
            diag_new[:, lanes], state = adagrad(diag[:, lanes], rstate_ref[lanes].reshape(1, 128), grad)
            rstate_new[lanes] = state.reshape(128)
        if i % (9 // PARTS) == 9 // PARTS - 1:
            stores[2 + i // (9 // PARTS)].start()
    loads[4].wait()
    first_new[...], fstate_new[...] = adagrad(first[...], fstate_ref[...], fgrad[...])
    stores[0].start()
    loads[5].wait()
    second_new[...], sstate_new[...] = adagrad(second[...], sstate_ref[...], sgrad[...])
    stores[1].start()
    for store in stores:
        store.wait()


def update_call(rel_grad, diag, rstate, first, fstate, first_grad, second, sstate, second_grad):
    shape = jax.ShapeDtypeStruct
    vmem, hbm = pl.BlockSpec(memory_space=pltpu.VMEM), pl.BlockSpec(memory_space=pltpu.HBM)
    table = pltpu.VMEM((D, R), F32)
    return pl.pallas_call(
        update_kernel,
        out_shape=(
            shape((D, K), F32), shape((K,), F32), shape((D, R), F32), shape((1, R), F32),
            shape((D, R), F32), shape((1, R), F32),
        ),
        in_specs=[hbm, vmem, vmem, vmem, vmem, hbm, vmem, vmem, hbm],
        out_specs=(hbm, vmem, hbm, vmem, hbm, vmem),
        scratch_shapes=[
            pltpu.VMEM((2 * H_CORE, 128), BF16), table, table, pltpu.VMEM((D, K), F32), table, table,
            pltpu.SemaphoreType.DMA((6,)), pltpu.SemaphoreType.DMA((2 + PARTS,)),
        ],
        compiler_params=pltpu.CompilerParams(vmem_limit_bytes=24 * 1024 * 1024),
        name="table_update",
    )(rel_grad, diag, rstate, first, fstate, first_grad, second, sstate, second_grad)


def on_device(
    first_table, first_state, second_table, second_state, relation_diag, relation_state,
    source_row, target_owner, target_row, relation_id, negative_id,
):
    diag, first, second = relation_diag.T, first_table[0].T, second_table[0].T
    first_grad, second_grad, rel_grad = step_call(
        first, second, diag,
        source_row, target_owner.reshape(1, E), target_row, relation_id, negative_id[0],
    )
    first_grad, second_grad, rel_grad = (
        pltpu.with_memory_space_constraint(v, pltpu.HBM) for v in (first_grad, second_grad, rel_grad)
    )
    diag_new, state_new, first_new, first_state_new, second_new, second_state_new = update_call(
        rel_grad, diag, relation_state, first, first_state, first_grad, second, second_state, second_grad
    )
    return (
        first_new.T[None], first_state_new, second_new.T[None], second_state_new,
        diag_new.T, state_new,
    )


def solution(mesh):
    in_specs = (
        P("group", "owner", None),
        P("group", "owner"),
        P("group", "owner", None),
        P("group", "owner"),
        P(),
        P(),
        P("group", "owner"),
        P("group", "owner", None),
        P("group", "owner"),
        P("group", "owner"),
        P("group", None, None),
    )
    out_specs = (
        P("group", "owner", None),
        P("group", "owner"),
        P("group", "owner", None),
        P("group", "owner"),
        P(),
        P(),
    )
    return jax.shard_map(
        on_device, mesh=mesh, in_specs=in_specs, out_specs=out_specs, check_vma=False
    )
```
